512 devices in a mesh: roll: 64 (over x, z, core), side: 8 (over y).
Axes of the slice: x: 4, y: 8, z: 8, core: 2. Of those that a mesh axis runs over, the one named last changes fastest.
Arguments:
- pressure: float32 [8192, 2048], P('roll', 'side'), may hold values from -6 to 6
- source: float32 [8192, 2048], P('roll', 'side'), may hold values from -6 to 6
- side_coupling: float32 [8192, 2048], P('roll', 'side'), may hold values from 0.4 to 0.8
- block_inverse: float32 [8192, 1024], P('roll', 'side'), may hold values from -1 to 1
- lower_coupling: float32 [64, 2048], P('roll', 'side'), may hold values from 0.5 to 30
- cavity_mask: int32 [64, 2048], P('roll', 'side'), may hold values 0 or 1
- rough_code: int32 [8192, 2048], P('roll', 'side'), may hold values from 0 to 15
- film_offset: float32 [1], replicated, may hold values from 0.5 to 1.5
Outputs:
- new_pressure: float32 [8192, 2048], P('roll', 'side')
- film: float32 [8192, 2048], P('roll', 'side')
The draws below stay inside these ranges and needn't reach their ends.
All inputs are finite; a program needn't handle non-finite values. No bound on the sum of `cavity_mask` on one device may be relied on, other than what follows from the above.
Results may differ from the reference program's by a relative error of at most 0.00018.
Values sent between devices are 32-bit elements; how exact they have to be, the bound alone decides.
A program may use at most 64 MiB of HBM per device.

```python
import math
import jax
import jax.numpy as jnp
from jax import lax

SECTION = 128
COLUMNS = 256
SWEEPS = 4
SECTIONS = 64
GRID_X = 8192
GRID_Y = 2048
FFT_X = 16384
FFT_Y = 4096
N_ROLL = 64
N_SIDE = 8


def corner_table(key):
    return 0.05 * jax.random.uniform(jax.random.fold_in(key, 7), (N_ROLL, N_SIDE), jnp.float32, 0.8, 1.2)


def draw_block_inverse(key, part):
    mesh_dimensions = (GRID_X, SECTION * N_SIDE)
    row_index = jnp.arange(GRID_X, dtype=jnp.int32)[:, None]
    column_index = jnp.arange(SECTION * N_SIDE, dtype=jnp.int32)[None, :]
    inner_row = row_index % SECTION
    inner_col = column_index % SECTION
    spread = jax.random.truncated_normal(jax.random.fold_in(key, 11), -4.0, 4.0, mesh_dimensions, jnp.float32) * (0.3 / math.sqrt(SECTION))
    diagonal = jax.random.uniform(jax.random.fold_in(key, 12), mesh_dimensions, jnp.float32, 0.5, 1.0)
    values = jnp.where(inner_row == inner_col, diagonal, spread)
    values = jnp.where(inner_col == 0, 0.05 * values, values)
    values = jnp.where(inner_row == SECTION - 1, 0.05 * values, values)
    corners = corner_table(key)[row_index // SECTION, column_index // SECTION]
    return jnp.where((inner_row == SECTION - 1) & (inner_col == 0), corners, values)


def draw_lower_coupling(key, part):
    mesh_dimensions = (N_ROLL, GRID_Y)
    segment_index = jnp.arange(N_ROLL, dtype=jnp.int32)[:, None]
    column_index = jnp.arange(GRID_Y, dtype=jnp.int32)[None, :]
    slow_share = 0.5
    sluggish_marker = jax.random.uniform(jax.random.fold_in(key, 21), (1, GRID_Y), jnp.float32) < slow_share
    sluggish_speed = jnp.exp(jax.random.uniform(jax.random.fold_in(key, 22), mesh_dimensions, jnp.float32, math.log(0.15), math.log(0.6))) * (2.3 / N_ROLL)
    quick_speed = jax.random.uniform(jax.random.fold_in(key, 23), mesh_dimensions, jnp.float32, 1.0, 3.0)
    placement_slots = jax.random.randint(jax.random.fold_in(key, 24), (2, GRID_Y), 0, N_ROLL)
    surge_marker = (segment_index == placement_slots[0:1]) | (segment_index == placement_slots[1:2])
    surge_penalty = jax.random.uniform(jax.random.fold_in(key, 25), mesh_dimensions, jnp.float32, 0.5, 0.8)
    retain_fraction = jnp.where(sluggish_marker, jnp.exp(-sluggish_speed) * jnp.where(surge_marker, surge_penalty, 1.0), jnp.exp(-quick_speed))
    corners = corner_table(key)[segment_index, column_index // COLUMNS]
    return retain_fraction / corners


def draw_source(key, part):
    mesh_dimensions = (GRID_X, GRID_Y)
    return jax.random.truncated_normal(jax.random.fold_in(key, 31), -6.0, 6.0, mesh_dimensions, jnp.float32)


def touch_ends(values, key, least, high):
    longest = values.shape.index(max(values.shape))
    spots = []
    for shift in (0, 1):
        where = [jax.random.randint(jax.random.fold_in(key, axis), (), 0, length) for axis, length in enumerate(values.shape)]
        where[longest] = (where[longest] + shift) % values.shape[longest]
        spots.append(tuple(where))
    return values.at[spots[0]].set(least).at[spots[1]].set(high)


def level_of(stream_key, extent, pieces, least, top_value):
    level, own = 1.0, jax.random.fold_in(stream_key, 6)
    for axis_at, parts in pieces:
        draws = jnp.exp(jax.random.uniform(jax.random.fold_in(own, axis_at), (parts,), jnp.float32, least / len(pieces), top_value / len(pieces)))
        level = level * jnp.repeat(draws, extent[axis_at] // parts).reshape([-1 if axis == axis_at else 1 for axis in range(len(extent))])
    return level


def bell_draw(own_key, extent, width, bound, pieces=(), kind=jnp.bfloat16):
    values = width * jax.random.normal(own_key, extent, jnp.float32)
    if pieces:
        values = values * level_of(own_key, extent, pieces, -0.22, 0.18)
    return jnp.clip(values, -bound, bound).astype(kind)


def setup_inputs(seed: int = 0) -> dict:
    streams_of = jax.random.split(jax.random.key(seed), 9)
    pressure = bell_draw(streams_of[0], (GRID_X, GRID_Y), 1.0, 6.0, ((0, 64), (1, 8)), jnp.float32)
    source = draw_source(jax.random.fold_in(streams_of[8], 71), 0)
    side_coupling = jnp.clip(jnp.exp(math.log(0.8) - 0.6931472 * jax.random.uniform(streams_of[2], (GRID_X, GRID_Y), jnp.float32) ** level_of(streams_of[2], (GRID_X, GRID_Y), ((0, 64), (1, 8)), -0.2, 0.2)), 0.4, 0.8)
    block_inverse = draw_block_inverse(jax.random.fold_in(streams_of[8], 71), 0)
    lower_coupling = draw_lower_coupling(jax.random.fold_in(streams_of[8], 71), 0)
    cavity_mask = touch_ends((jax.random.randint(streams_of[5], (SECTIONS, GRID_Y), 0, 2) < 1).astype(jnp.int32), jax.random.fold_in(streams_of[5], 1), 0, 1)
    rough_code = touch_ends(jax.random.randint(streams_of[6], (GRID_X, GRID_Y), 0, 16), jax.random.fold_in(streams_of[6], 1), 0, 15).astype(jnp.int32)
    film_offset = jnp.clip(jax.random.uniform(streams_of[7], (1,), jnp.float32, 0.5, 1.5), 0.5, 1.5)
    return dict(pressure=pressure, source=source, side_coupling=side_coupling, block_inverse=block_inverse, lower_coupling=lower_coupling, cavity_mask=cavity_mask, rough_code=rough_code, film_offset=film_offset)


HIGHEST = lax.Precision.HIGHEST
ROUGH_STEP = 0.05

def relax_sweep(pressure_now, source, side_coupling, inverses, lower_blocks, mask_on):
    padded = jnp.pad(pressure_now, ((0, 0), (1, 1)))
    right_side = source + side_coupling * (padded[:, :-2] + padded[:, 2:])
    blocks = right_side.reshape(N_ROLL, SECTION, N_SIDE, COLUMNS)
    line_local = jnp.einsum('kism,kmsc->kisc', inverses, blocks, precision=HIGHEST)
    gain_rows = inverses[:, SECTION - 1, :, 0][:, :, None] * lower_blocks

    def advance(carry_in, inputs):
        outflow, gain_value = inputs
        return (outflow + gain_value * carry_in, carry_in)
    start_carry = jnp.zeros((N_SIDE, COLUMNS), jnp.float32)
    final_carry, carries = lax.scan(advance, start_carry, (line_local[:, SECTION - 1], gain_rows))
    solved = line_local + inverses[:, :, :, 0][..., None] * (lower_blocks * carries)[:, None]
    solved = jnp.where(mask_on, jnp.maximum(solved, 0.0), solved)
    return solved.reshape(GRID_X, GRID_Y)

def elastic_deflection(pressure_now):
    row_freq = jnp.arange(FFT_X, dtype=jnp.int32)
    col_freq = jnp.arange(FFT_Y // 2 + 1, dtype=jnp.int32)
    row_wave = jnp.minimum(row_freq, FFT_X - row_freq).astype(jnp.float32) / FFT_X
    col_wave = col_freq.astype(jnp.float32) / FFT_Y
    kernel_reach = min(FFT_X, FFT_Y) / 16.0
    radius = jnp.sqrt(row_wave[:, None] * row_wave[:, None] + col_wave[None, :] * col_wave[None, :])
    kernel = 0.4 * kernel_reach / (1.0 + kernel_reach * radius)
    spectrum = jnp.fft.rfft2(pressure_now, s=(FFT_X, FFT_Y))
    return jnp.fft.irfft2(spectrum * kernel, s=(FFT_X, FFT_Y))[:GRID_X, :GRID_Y]

def reference(pressure, source, side_coupling, block_inverse, lower_coupling, cavity_mask, rough_code, film_offset):
    inverses = block_inverse.reshape(N_ROLL, SECTION, N_SIDE, SECTION)
    lower_blocks = lower_coupling.reshape(N_ROLL, N_SIDE, COLUMNS)
    mask_on = (cavity_mask == 1).reshape(N_ROLL, 1, N_SIDE, COLUMNS)
    pressure_now = pressure
    for sweep_step in range(SWEEPS):
        pressure_now = relax_sweep(pressure_now, source, side_coupling, inverses, lower_blocks, mask_on)
    deflection = elastic_deflection(pressure_now)
    across = 4.0 * (jnp.arange(GRID_X).astype(jnp.float32) + 0.5) / GRID_X - 2.5
    transverse = 4.0 * (jnp.arange(GRID_Y).astype(jnp.float32) + 0.5) / GRID_Y - 2.0
    film_height = film_offset[0] + 0.5 * across[:, None] * across[:, None] + 0.5 * transverse[None, :] * transverse[None, :] + deflection - ROUGH_STEP * rough_code.astype(jnp.float32)
    return (pressure_now, film_height)
```

```python
import functools
import math

import jax
import jax.numpy as jnp
import ml_dtypes
import numpy as np
from jax import lax
from jax.experimental import pallas as pl
from jax.experimental.pallas import tpu as pltpu
from jax.sharding import PartitionSpec as P

SWEEPS = 4
ROUGH_STEP = 0.05
MESH = pl.DeviceIdType.MESH
F32 = jnp.float32
BF16 = jnp.bfloat16

N_ROLL, N_SIDE = 64, 8
ROWS, COLS = 128, 256
FFT_X, FFT_Y = 2 * N_ROLL * ROWS, 2 * N_SIDE * COLS
CLASSES = N_SIDE + 1


def split_np(x):
    x = x.astype(np.float32)
    hi = x.astype(ml_dtypes.bfloat16)
    lo = (x - hi.astype(np.float32)).astype(ml_dtypes.bfloat16)
    return hi, lo


def wide_np(x, axis):
    hi, lo = split_np(x)
    return np.concatenate([hi, hi, lo], axis=axis)


def turns(ints, length):
    return 2.0 * np.pi * (ints % length).astype(np.float64) / length


@functools.lru_cache(None)
def tables():
    a = np.arange(N_ROLL)
    ang = turns(a[:, None] * a[None, :], 2 * N_ROLL)
    sect = np.stack([np.cos(ang), -np.sin(ang)], axis=1)
    sect[0, 1] = np.where(a % 2 == 0, 1.0, -1.0)
    sect = np.einsum("uca,ij->uciaj", sect, np.eye(4)).reshape(8 * N_ROLL, 4 * N_ROLL)
    c = np.arange(COLS)
    ang = turns(c[:, None] * c[None, :], COLS)
    dcos, dsin = np.cos(ang), np.sin(ang)
    dft = np.block([[dcos, -dsin], [dsin, dcos]])
    v1 = np.arange(16)
    ang = turns(v1[:, None] * c[None, :], FFT_Y)
    twiddle = np.stack([np.cos(ang), np.sin(ang)]).astype(np.float32)
    q = np.arange(ROWS).reshape(N_SIDE, 16)
    t = np.arange(ROWS).reshape(32, 4)
    ang = turns(q[:, :, None, None] * t[None, None], ROWS)
    cb, sb = np.cos(ang), np.sin(ang)
    main = np.zeros((2, 2, N_SIDE, 2, 16, 32, 2, 4))
    main[1, 0, :, 0, :, :, 0], main[1, 0, :, 0, :, :, 1] = cb, sb
    main[1, 0, :, 1, :, :, 0], main[1, 0, :, 1, :, :, 1] = -sb, cb
    main[1, 1, :, 0, :, :, 0], main[1, 1, :, 0, :, :, 1] = -sb, cb
    main[1, 1, :, 1, :, :, 0], main[1, 1, :, 1, :, :, 1] = -cb, -sb
    even = np.where(q <= 64, q, q - 64)
    ang = turns(even[:, :, None, None] * t[None, None], ROWS)
    main[0, 0, :, 0, :, :, 0] = np.where((q <= 64)[:, :, None, None], np.cos(ang), np.sin(ang))
    odd = 64 + 128 * np.where(q < 64, q, q - 64)
    ang = turns(odd[:, :, None, None] * t[None, None], FFT_X)
    main[0, 0, :, 1, :, :, 1] = np.where((q < 64)[:, :, None, None], np.cos(ang), np.sin(ang))
    main = main.reshape(2, 2, 256, 256).astype(np.float32)
    cols_t = np.broadcast_to(t[:, None, :], (32, 2, 4)).reshape(256)
    ang = turns(a[:, None] * cols_t[None, :], FFT_X)
    slant = np.stack([np.cos(ang), np.sin(ang)], axis=1).astype(np.float32)
    return (
        wide_np(sect, 1),
        wide_np(sect.T, 1),
        wide_np(dft, 0),
        wide_np(dft.T, 0),
        main,
        slant,
        twiddle,
    )


def split(x):
    hi = x.astype(BF16)
    return hi, (x - hi.astype(F32)).astype(BF16)


def mm(a, b):
    return jnp.dot(a, b, preferred_element_type=F32)


def place(device):
    return lax.rem(device, 2) * 32 + lax.div(device, 2)


def combine(terms):
    total = None
    for coef, value in terms:
        if abs(coef) < 1e-12:
            continue
        if abs(coef - 1.0) < 1e-12:
            total = value if total is None else total + value
        elif abs(coef + 1.0) < 1e-12:
            total = -value if total is None else total - value
        else:
            total = coef * value if total is None else total + coef * value
    return total


def main_kernel(
    press, source, coupling, binv, lower, mask, rough, offset,
    w3_h, wt3_h, d3_h, dt3_h, main_h, slant_h, twid_h,
    newp, film,
    w3, wt3, d3, dt3, maint, slant, twid,
    pack, halo, bhalo,
    outs0, outs, recv0, recv, carry_buf,
    b3, be3,
    kern, m3, mt3,
    p1s, p1r, q3, p2s, p2r, x3, us, yb, zs, ob, ub, p5s, p5r, v3, p6s, p6r,
    const_sem, halo_ss, halo_rs, ss, rs,
):
    me = lax.axis_index("roll")
    side = lax.axis_index("side")
    barrier = pltpu.get_barrier_semaphore()

    def sig_roll(d, _):
        pl.semaphore_signal(
            barrier, inc=1, device_id={"roll": lax.rem(me + d, N_ROLL)}, device_id_type=MESH
        )
        return 0

    def sig_side(d, _):
        pl.semaphore_signal(
            barrier, inc=1, device_id={"side": lax.rem(side + d, N_SIDE)}, device_id_type=MESH
        )
        return 0

    lax.fori_loop(1, N_SIDE, sig_side, 0)
    lax.fori_loop(1, N_ROLL, sig_roll, 0)

    variant = jnp.minimum(me, 1)
    loads = [
        pltpu.make_async_copy(s, d, const_sem.at[i])
        for i, (s, d) in enumerate(
            [
                (w3_h, w3), (wt3_h, wt3), (d3_h, d3), (dt3_h, dt3),
                (main_h.at[variant], maint), (slant_h.at[me], slant), (twid_h, twid),
            ]
        )
    ]
    for load in loads:
        load.start()

    def send_all(axis, n, mine, src_at, dst_at, phase):
        def body(d, _):
            to = lax.rem(mine + d, n)
            pltpu.make_async_remote_copy(
                src_ref=src_at(to), dst_ref=dst_at(mine), send_sem=ss.at[phase],
                recv_sem=rs.at[phase], device_id={axis: to}, device_id_type=MESH,
            ).start()
            return 0

        lax.fori_loop(1, n, body, 0)

    def wait_all(axis, n, mine, src, dst, phase):
        c = pltpu.make_async_remote_copy(
            src_ref=src, dst_ref=dst, send_sem=ss.at[phase], recv_sem=rs.at[phase],
            device_id={axis: lax.rem(mine + 1, n)}, device_id_type=MESH,
        )
        c.wait()

    lane_b = lax.broadcasted_iota(jnp.int32, (ROWS, 128), 1)
    for i, ref in enumerate((press, source, coupling)):
        pack[0, pl.ds(8 * i, 8), :] = ref[:, 0:128].T[0:8]
        pack[1, pl.ds(8 * i, 8), :] = ref[:, 128:256].T[120:128]
    for j in range(2):
        lanes = slice(128 * j, 128 * j + 128)
        pack[j, pl.ds(24, 8), :] = jnp.concatenate(
            [lower[:, lanes], mask[:, lanes].astype(F32), jnp.zeros((6, 128), F32)], axis=0
        )
    pl.semaphore_wait(barrier, N_ROLL + N_SIDE - 2)
    halo_copies = []
    for j, d in ((0, N_SIDE - 1), (1, 1)):
        to = lax.rem(side + d, N_SIDE)
        for k, (s, dst) in enumerate(((pack.at[j], halo.at[j]), (binv, bhalo.at[j]))):
            c = pltpu.make_async_remote_copy(
                src_ref=s, dst_ref=dst, send_sem=halo_ss.at[j, k], recv_sem=halo_rs.at[j, k],
                device_id={"side": to}, device_id_type=MESH,
            )
            c.start()
            halo_copies.append(c)
    bhi, blo = split(binv[...])
    b3[:, 0:128] = bhi
    b3[:, 128:256] = bhi
    b3[:, 256:384] = blo
    for c in halo_copies:
        c.wait()
    has_right = side < N_SIDE - 1
    has_left = side > 0
    is_right = lane_b < 64
    valid = jnp.logical_or(
        jnp.logical_and(is_right, has_right), jnp.logical_and(jnp.logical_not(is_right), has_left)
    )
    ext = []
    for i in range(3):
        tall = jnp.concatenate(
            [halo[0, pl.ds(8 * i, 8), :], jnp.zeros((112, 128), F32), halo[1, pl.ds(8 * i, 8), :]],
            axis=0,
        )
        ext.append(jnp.where(valid, tall.T, 0.0))
    row_right = is_right[0:1]
    row_valid = valid[0:1]
    lower_e = jnp.where(row_valid, jnp.where(row_right, halo[0, 24:25, :], halo[1, 24:25, :]), 0.0)
    mask_e = jnp.where(row_right, halo[0, 25:26, :], halo[1, 25:26, :]) > 0.5
    rhi, rlo = split(bhalo[0])
    lhi, llo = split(bhalo[1])
    for i, part in enumerate((rhi, lhi, rhi, lhi, rlo, llo)):
        be3[:, pl.ds(128 * i, 128)] = part
    first_e = jnp.where(is_right, bhalo[0, :, 0:1], bhalo[1, :, 0:1])
    first = binv[:, 0:1]
    gain_e = first_e[127:128] * lower_e
    gain_m = binv[127:128, 0:1] * lower[...]
    lower_w = jnp.concatenate([lower[...], lower_e], axis=1)
    mask_w = jnp.concatenate([mask[...].astype(F32), mask_e.astype(F32)], axis=1) > 0.5
    first_w = jnp.concatenate([jnp.broadcast_to(first, (ROWS, COLS)), first_e], axis=1)
    source_w = jnp.concatenate([source[...], ext[1]], axis=1)
    coupling_w = jnp.concatenate([coupling[...], ext[2]], axis=1)
    field = jnp.concatenate([press[...], ext[0]], axis=1)
    for i in range(3):
        gi = gain_e if i == 2 else gain_m[:, 128 * i : 128 * i + 128]
        outs0[1, i : i + 1, :] = gi

    for sweep in range(SWEEPS):
        rhs = source_w + coupling_w * (pltpu.roll(field, 1, 1) + pltpu.roll(field, 383, 1))
        hi, lo = split(rhs)
        stack = jnp.concatenate([hi[:, :256], lo[:, :256], hi[:, :256]], axis=0)
        he, le = rhs[:, 256:], None
        hr, lr = split(jnp.where(is_right, he, 0.0))
        hl, ll = split(jnp.where(is_right, 0.0, he))
        stack_e = jnp.concatenate([hr, hl, lr, ll, hr, hl], axis=0)
        tail = mm(b3[112:128, :], stack)
        tail_e = mm(be3[112:128, :], stack_e)
        for i in range(3):
            row = tail_e[15:16] if i == 2 else tail[15:16, 128 * i : 128 * i + 128]
            if sweep == 0:
                outs0[0, i : i + 1, :] = row
            else:
                outs[sweep - 1, i : i + 1, :] = row
        if sweep == 0:
            send_all("roll", N_ROLL, me, lambda to: outs0, lambda m: recv0.at[m], 0)
        else:
            send_all(
                "roll", N_ROLL, me, lambda to: outs.at[sweep - 1],
                lambda m: recv.at[sweep - 1, m], sweep,
            )
        local = jnp.concatenate([mm(b3[...], stack), mm(be3[...], stack_e)], axis=1)
        if sweep == 0:
            i = lax.broadcasted_iota(jnp.int32, (32, COLS), 0)
            q = 16 * side + jnp.where(i < 16, i, i - 16)
            low_part = i < 16
            u_even = 128 * jnp.where(q <= 64, q, q - 64)
            u_odd = 64 + 128 * jnp.where(q < 64, q, q - 64)
            u = jnp.where(me == 0, jnp.where(low_part, u_even, u_odd), me + 128 * q)
            fu = jnp.minimum(u, FFT_X - u).astype(F32) / FFT_X
            single = jnp.logical_and(
                jnp.logical_and(me == 0, low_part), jnp.logical_or(q == 0, q == 64)
            )
            reach = min(FFT_X, FFT_Y) / 16.0
            scale = 0.4 * reach / (float(FFT_X) * float(FFT_Y))
            weight = jnp.where(single, scale, 2.0 * scale)
            fu2 = fu * fu
            lane = lax.broadcasted_iota(jnp.int32, (32, COLS), 1)
            for v1 in range(CLASSES):
                v = v1 + 16 * lane
                fv = jnp.minimum(v, FFT_Y - v).astype(F32) / FFT_Y
                w = weight if v1 in (0, 8) else 2.0 * weight
                kern[pl.ds(32 * v1, 32), :] = w / (1.0 + reach * jnp.sqrt(fu2 + fv * fv))
        if sweep == 1:
            loads[4].wait()
            loads[5].wait()
            mrow = maint[0] * slant[0:1, :] + maint[1] * slant[1:2, :]
            hi, lo = split(mrow)
            m3[:, 0:256] = hi
            m3[:, 256:512] = hi
            m3[:, 512:768] = lo
        if sweep == 2:
            mrow = maint[0] * slant[0:1, :] + maint[1] * slant[1:2, :]
            hi, lo = split(mrow.T)
            mt3[:, 0:256] = hi
            mt3[:, 256:512] = hi
            mt3[:, 512:768] = lo
        if sweep == 0:
            wait_all(
                "roll", N_ROLL, me, recv0.at[pl.ds(0, N_ROLL - 1)],
                recv0.at[pl.ds(0, N_ROLL - 1)], 0,
            )
        else:
            sl = recv.at[sweep - 1, pl.ds(0, N_ROLL - 1)]
            wait_all("roll", N_ROLL, me, sl, sl, sweep)

        def advance(k8, c):
            for j in range(8):
                k = 8 * k8 + j
                carry_buf[k] = c
                flow = recv0[k, 0] if sweep == 0 else recv[sweep - 1, k]
                c = flow + recv0[k, 1] * c
            return c

        lax.fori_loop(0, N_ROLL // 8, advance, jnp.zeros((3, 128), F32))
        mine = carry_buf[me]
        carry = jnp.concatenate([mine[0:1], mine[1:2], mine[2:3]], axis=1)
        solved = local + first_w * (lower_w * carry)
        field = jnp.where(mask_w, jnp.maximum(solved, 0.0), solved)

    result = field[:, :COLS]
    newp[...] = result

    for h in range(2):
        p1s[pl.ds(32 * h, 32)] = result[:, 128 * h : 128 * h + 128].reshape(32, 4, 128)
    send_all("roll", N_ROLL, me, lambda to: p1s.at[place(to)], lambda m: p1r.at[m], 4)
    p1r[me] = p1s[place(me)]
    loads[0].wait()
    wait_all("roll", N_ROLL, me, p1s.at[pl.ds(0, 63)], p1r.at[pl.ds(0, 63)], 4)
    hi, lo = split(p1r[...].reshape(256, 128))
    q3[0:256] = hi
    q3[256:512] = lo
    q3[512:768] = hi
    p2s[...] = mm(w3[...], q3[...]).reshape(64, 8, 128)

    send_all("roll", N_ROLL, me, lambda to: p2s.at[to], lambda m: p2r.at[place(m)], 5)
    p2r[place(me)] = p2s[me]
    wait_all("roll", N_ROLL, me, p2s.at[pl.ds(0, 63)], p2r.at[pl.ds(0, 63)], 5)
    for h in range(2):
        hi, lo = split(p2r[pl.ds(32 * h, 32)].reshape(256, 128))
        lanes = slice(128 * h, 128 * h + 128)
        x3[0:256, lanes] = hi
        x3[256:512, lanes] = lo
        x3[512:768, lanes] = hi
    us[...] = mm(m3[...], x3[...]).reshape(8, 32, 256)

    send_all("side", N_SIDE, side, lambda to: us.at[to], lambda m: yb.at[m], 6)
    yb[side] = us[side]
    loads[2].wait()
    loads[3].wait()
    loads[6].wait()
    wait_all("side", N_SIDE, side, us.at[pl.ds(0, 7)], yb.at[pl.ds(0, 7)], 6)

    cosines = [[math.cos(math.pi * s * v / 8.0) for v in range(9)] for s in range(8)]
    sines = [[math.sin(math.pi * s * v / 8.0) for v in range(9)] for s in range(8)]

    def put(v1, rows, lanes, re, im):
        at = 32 * v1 + rows
        for part, value in ((0, re), (256, im)):
            hi, lo = split(value)
            zs[pl.ds(at, 16), pl.ds(part + lanes, 128)] = hi
            zs[pl.ds(at, 16), pl.ds(512 + part + lanes, 128)] = lo
            zs[pl.ds(at, 16), pl.ds(1024 + part + lanes, 128)] = hi

    for rows in (0, 16):
        for lanes in (0, 128):
            x = [yb[s, pl.ds(rows, 16), pl.ds(lanes, 128)] for s in range(8)]
            for v in range(5):
                er = combine([(cosines[s][v], x[s]) for s in (0, 2, 4, 6)])
                orr = combine([(cosines[s][v], x[s]) for s in (1, 3, 5, 7)])
                ei = combine([(-sines[s][v], x[s]) for s in (0, 2, 4, 6)])
                oi = combine([(-sines[s][v], x[s]) for s in (1, 3, 5, 7)])
                zero = jnp.zeros((16, 128), F32)
                ei = zero if ei is None else ei
                oi = zero if oi is None else oi
                orr = zero if orr is None else orr
                todo = [(v, er + orr, ei + oi)]
                if v < 4:
                    todo.append((8 - v, er - orr, oi - ei))
                for v1, yr, yi in todo:
                    c = twid[0, v1 : v1 + 1, lanes : lanes + 128]
                    s = twid[1, v1 : v1 + 1, lanes : lanes + 128]
                    put(v1, rows, lanes, yr * c + yi * s, yi * c - yr * s)
    spec = mm(zs[...], d3[...])
    for v1 in range(CLASSES):
        for rows in (0, 16):
            at = 32 * v1 + rows
            for lanes in (0, 128):
                k = kern[pl.ds(at, 16), pl.ds(lanes, 128)]
                put(
                    v1, rows, lanes,
                    spec[at : at + 16, lanes : lanes + 128] * k,
                    spec[at : at + 16, 256 + lanes : 384 + lanes] * k,
                )
    back = mm(zs[...], dt3[...])
    for rows in (0, 16):
        for lanes in (0, 128):
            yr, yi = [], []
            for v1 in range(CLASSES):
                at = 32 * v1 + rows
                zr = back[at : at + 16, lanes : lanes + 128]
                zi = back[at : at + 16, 256 + lanes : 384 + lanes]
                c = twid[0, v1 : v1 + 1, lanes : lanes + 128]
                s = twid[1, v1 : v1 + 1, lanes : lanes + 128]
                yr.append(zr * c - zi * s)
                yi.append(zr * s + zi * c)
            plus_r = [yr[v] + yr[8 - v] for v in range(4)] + [yr[4]]
            plus_i = [yi[v] + yi[8 - v] for v in range(4)] + [yi[4]]
            less_r = [yr[v] - yr[8 - v] for v in range(4)] + [yr[4]]
            less_i = [yi[v] - yi[8 - v] for v in range(4)] + [yi[4]]
            for s in range(8):
                re, im = (plus_r, less_i) if s % 2 == 0 else (less_r, plus_i)
                ob[s, pl.ds(rows, 16), pl.ds(lanes, 128)] = combine(
                    [(cosines[s][v], re[v]) for v in range(5)]
                    + [(-sines[s][v], im[v]) for v in range(5)]
                )

    send_all("side", N_SIDE, side, lambda to: ob.at[to], lambda m: ub.at[m], 7)
    ub[side] = ob[side]
    wait_all("side", N_SIDE, side, ob.at[pl.ds(0, 7)], ub.at[pl.ds(0, 7)], 7)
    hi, lo = split(ub[...].reshape(256, 256))
    x3[0:256] = hi
    x3[256:512] = lo
    x3[512:768] = hi
    rows_back = mm(mt3[...], x3[...])
    for h in range(2):
        p5s[pl.ds(32 * h, 32)] = rows_back[:, 128 * h : 128 * h + 128].reshape(32, 8, 128)

    send_all("roll", N_ROLL, me, lambda to: p5s.at[place(to)], lambda m: p5r.at[m], 8)
    p5r[me] = p5s[place(me)]
    loads[1].wait()
    wait_all("roll", N_ROLL, me, p5s.at[pl.ds(0, 63)], p5r.at[pl.ds(0, 63)], 8)
    hi, lo = split(p5r[...].reshape(512, 128))
    v3[0:512] = hi
    v3[512:1024] = lo
    v3[1024:1536] = hi
    p6s[...] = mm(wt3[...], v3[...]).reshape(64, 4, 128)

    send_all("roll", N_ROLL, me, lambda to: p6s.at[to], lambda m: p6r.at[place(m)], 9)
    p6r[place(me)] = p6s[me]
    row_pos = (me * ROWS + lax.broadcasted_iota(jnp.int32, (ROWS, COLS), 0)).astype(F32)
    col_pos = (side * COLS + lax.broadcasted_iota(jnp.int32, (ROWS, COLS), 1)).astype(F32)
    across = 4.0 * (row_pos + 0.5) / (ROWS * N_ROLL) - 2.5
    transverse = 4.0 * (col_pos + 0.5) / (COLS * N_SIDE) - 2.0
    ground = offset[0] + 0.5 * across * across + 0.5 * transverse * transverse
    ripple = ROUGH_STEP * rough[...].astype(F32)
    wait_all("roll", N_ROLL, me, p6s.at[pl.ds(0, 63)], p6r.at[pl.ds(0, 63)], 9)
    for h in range(2):
        lanes = slice(128 * h, 128 * h + 128)
        bend = p6r[pl.ds(32 * h, 32)].reshape(128, 128)
        film[:, lanes] = ground[:, lanes] + bend - ripple[:, lanes]


def per_device(pressure, source, coupling, binv, lower, mask, rough, offset):
    consts = [jnp.asarray(t) for t in tables()]
    vm = pl.BlockSpec(memory_space=pltpu.VMEM)
    hbm = pl.BlockSpec(memory_space=pl.ANY)
    f = lambda *shape: pltpu.VMEM(shape, F32)
    b = lambda *shape: pltpu.VMEM(shape, BF16)
    scratch = [
        b(512, 768), b(256, 1536), b(1536, 512), b(1536, 512),
        f(2, 256, 256), f(2, 256), f(2, 16, 256),
        f(2, 32, 128), f(2, 32, 128), f(2, 128, 128),
        f(2, 3, 128), f(3, 3, 128), f(64, 2, 3, 128), f(3, 64, 3, 128), f(64, 3, 128),
        b(128, 384), b(128, 768),
        f(288, 256), b(256, 768), b(256, 768),
        f(64, 4, 128), f(64, 4, 128), b(768, 128), f(64, 8, 128), f(64, 8, 128), b(768, 256),
        f(8, 32, 256), f(8, 32, 256), b(288, 1536), f(8, 32, 256), f(8, 32, 256),
        f(64, 8, 128), f(64, 8, 128), b(1536, 128), f(64, 4, 128), f(64, 4, 128),
        pltpu.SemaphoreType.DMA((7,)),
        pltpu.SemaphoreType.DMA((2, 2)), pltpu.SemaphoreType.DMA((2, 2)),
        pltpu.SemaphoreType.DMA((10,)), pltpu.SemaphoreType.DMA((10,)),
    ]
    out = jax.ShapeDtypeStruct((ROWS, COLS), F32)
    return pl.pallas_call(
        main_kernel,
        out_shape=(out, out),
        in_specs=[vm] * 7 + [pl.BlockSpec(memory_space=pltpu.SMEM)] + [hbm] * 7,
        out_specs=(vm, vm),
        scratch_shapes=scratch,
        compiler_params=pltpu.CompilerParams(
            collective_id=0, has_side_effects=True, vmem_limit_bytes=40 * 1024 * 1024
        ),
    )(pressure, source, coupling, binv, lower, mask, rough, offset, *consts)


def solution(mesh):
    spec = P("roll", "side")
    return jax.shard_map(
        per_device,
        mesh=mesh,
        in_specs=(spec,) * 7 + (P(),),
        out_specs=(spec, spec),
        check_vma=False,
    )
```

```python
import functools
import math

import jax
import jax.numpy as jnp
import ml_dtypes
import numpy as np
from jax import lax
from jax.experimental import pallas as pl
from jax.experimental.pallas import tpu as pltpu
from jax.sharding import PartitionSpec as P

SWEEPS = 4
ROUGH_STEP = 0.05
MESH = pl.DeviceIdType.MESH
F32 = jnp.float32
BF16 = jnp.bfloat16

N_ROLL, N_SIDE = 64, 8
ROWS, COLS = 128, 256
FFT_X, FFT_Y = 2 * N_ROLL * ROWS, 2 * N_SIDE * COLS
CLASSES = N_SIDE + 1


def split_np(x):
    x = x.astype(np.float32)
    hi = x.astype(ml_dtypes.bfloat16)
    lo = (x - hi.astype(np.float32)).astype(ml_dtypes.bfloat16)
    return hi, lo


def wide_np(x, axis):
    hi, lo = split_np(x)
    return np.concatenate([hi, hi, lo], axis=axis)


def turns(ints, length):
    return 2.0 * np.pi * (ints % length).astype(np.float64) / length


@functools.lru_cache(None)
def tables():
    a = np.arange(N_ROLL)
    ang = turns(a[:, None] * a[None, :], 2 * N_ROLL)
    sect = np.stack([np.cos(ang), -np.sin(ang)], axis=1)
    sect[0, 1] = np.where(a % 2 == 0, 1.0, -1.0)
    sect = np.einsum("uca,ij->uciaj", sect, np.eye(4)).reshape(8 * N_ROLL, 4 * N_ROLL)
    c = np.arange(COLS)
    ang = turns(c[:, None] * c[None, :], COLS)
    dcos, dsin = np.cos(ang), np.sin(ang)
    dft = np.block([[dcos, -dsin], [dsin, dcos]])
    v1 = np.arange(16)
    ang = turns(v1[:, None] * c[None, :], FFT_Y)
    twiddle = np.stack([np.cos(ang), np.sin(ang)]).astype(np.float32)
    q = np.arange(ROWS).reshape(N_SIDE, 16)
    t = np.arange(ROWS).reshape(32, 4)
    ang = turns(q[:, :, None, None] * t[None, None], ROWS)
    cb, sb = np.cos(ang), np.sin(ang)
    main = np.zeros((2, 2, 2, N_SIDE, 16, 32, 2, 4))
    main[1, 0, 0, :, :, :, 0], main[1, 0, 0, :, :, :, 1] = cb, sb
    main[1, 0, 1, :, :, :, 0], main[1, 0, 1, :, :, :, 1] = -sb, cb
    main[1, 1, 0, :, :, :, 0], main[1, 1, 0, :, :, :, 1] = -sb, cb
    main[1, 1, 1, :, :, :, 0], main[1, 1, 1, :, :, :, 1] = -cb, -sb
    even = np.where(q <= 64, q, q - 64)
    ang = turns(even[:, :, None, None] * t[None, None], ROWS)
    main[0, 0, 0, :, :, :, 0] = np.where((q <= 64)[:, :, None, None], np.cos(ang), np.sin(ang))
    odd = 64 + 128 * np.where(q < 64, q, q - 64)
    ang = turns(odd[:, :, None, None] * t[None, None], FFT_X)
    main[0, 0, 1, :, :, :, 1] = np.where((q < 64)[:, :, None, None], np.cos(ang), np.sin(ang))
    main = main.reshape(2, 2, 256, 256).astype(np.float32)
    cols_t = np.broadcast_to(t[:, None, :], (32, 2, 4)).reshape(256)
    ang = turns(a[:, None] * cols_t[None, :], FFT_X)
    slant = np.stack([np.cos(ang), np.sin(ang)], axis=1).astype(np.float32)
    return (
        wide_np(sect, 1),
        wide_np(sect.T, 1),
        wide_np(dft, 0),
        wide_np(dft.T, 0),
        main,
        slant,
        twiddle,
    )


def split(x):
    hi = x.astype(BF16)
    return hi, (x - hi.astype(F32)).astype(BF16)


def mm(a, b):
    return jnp.dot(a, b, preferred_element_type=F32)


def place(device):
    return lax.rem(device, 2) * 32 + lax.div(device, 2)


def combine(terms):
    total = None
    for coef, value in terms:
        if abs(coef) < 1e-12:
            continue
        if abs(coef - 1.0) < 1e-12:
            total = value if total is None else total + value
        elif abs(coef + 1.0) < 1e-12:
            total = -value if total is None else total - value
        else:
            total = coef * value if total is None else total + coef * value
    return total


def far(i, x, z, c):
    m, n = lax.div(i, 8), lax.div(lax.rem(i, 8), 2)
    dz = 4 + lax.div(m + 1, 2) * (1 - 2 * lax.rem(m, 2))
    dx = 2 + lax.div(n + 1, 2) * (1 - 2 * lax.rem(n, 2))
    return (
        lax.rem(x + dx, 4) * 16 + lax.rem(z + dz, 8) * 2 + lax.rem(c + 1 - lax.rem(i, 2), 2)
    )


def main_kernel(
    press_h, source_h, coupling_h, binv_h, lower_h, mask_h, rough_h, offset,
    w3_h, wt3_h, d3_h, dt3_h, main_h, slant_h, twid_h,
    newp_h, film_h,
    press, source, coupling, binv, lower, mask, rough, newp, film,
    w3, wt3, d3, dt3, maint, slant, twid,
    pack, halo, bhalo,
    cs, cr, outs0, outs, recv0, recv, gfull, carry_buf, gsel, bt, btt, bx, carry4, partner,
    b3, be3, loc4,
    kern, m3, mt3,
    p1s, p1r, qf, q3, p2s, p2r, x3, us, yb, zs, ob, ub, p5s, p5r, v3, p6s, p6r,
    const_sem, arg_sem, out_sem, halo_ss, halo_rs, ss, rs,
):
    me = lax.axis_index("roll")
    side = lax.axis_index("side")
    along_x, along_z, half = lax.div(me, 16), lax.rem(lax.div(me, 2), 8), lax.rem(me, 2)
    group = lax.div(me, 2)
    other = me + 1 - 2 * half
    barrier = pltpu.get_barrier_semaphore()

    def sig_roll(d, _):
        pl.semaphore_signal(
            barrier, inc=1, device_id={"roll": lax.rem(me + d, N_ROLL)}, device_id_type=MESH
        )
        return 0

    def sig_side(d, _):
        pl.semaphore_signal(
            barrier, inc=1, device_id={"side": lax.rem(side + d, N_SIDE)}, device_id_type=MESH
        )
        return 0

    lax.fori_loop(1, N_SIDE, sig_side, 0)
    lax.fori_loop(1, N_ROLL, sig_roll, 0)

    variant = jnp.minimum(me, 1)
    loads = [
        pltpu.make_async_copy(s, d, const_sem.at[i])
        for i, (s, d) in enumerate(
            [
                (w3_h, w3), (wt3_h, wt3), (d3_h, d3), (dt3_h, dt3),
                (main_h.at[variant], maint), (slant_h.at[me], slant), (twid_h, twid),
            ]
        )
    ]
    args = [
        pltpu.make_async_copy(s, d, arg_sem.at[i])
        for i, (s, d) in enumerate(
            [
                (press_h, press), (source_h, source), (coupling_h, coupling), (binv_h, binv),
                (lower_h, lower), (mask_h, mask), (rough_h, rough),
            ]
        )
    ]
    for load in args:
        load.start()
    for load in loads:
        load.start()

    def push(src, dst, phase, where):
        pltpu.make_async_remote_copy(
            src_ref=src, dst_ref=dst, send_sem=ss.at[phase], recv_sem=rs.at[phase],
            device_id=where, device_id_type=MESH,
        ).start()

    def send_roll(src_at, dst, phase):
        def body(i, _):
            to = far(i, along_x, along_z, half)
            push(src_at(to), dst, phase, {"roll": to})
            return 0

        lax.fori_loop(0, N_ROLL - 1, body, 0)

    def send_side(src_at, dst, phase):
        for d in (4, 3, 5, 2, 6, 1, 7):
            to = lax.rem(side + d, N_SIDE)
            push(src_at(to), dst, phase, {"side": to})

    def settle(src, dst, phase):
        pltpu.make_async_remote_copy(
            src_ref=src, dst_ref=dst, send_sem=ss.at[phase], recv_sem=rs.at[phase],
            device_id={"roll": other}, device_id_type=MESH,
        ).wait()

    rest = pl.ds(0, N_ROLL - 1)
    rest_side = pl.ds(0, N_SIDE - 1)

    lane_b = lax.broadcasted_iota(jnp.int32, (ROWS, 128), 1)
    for load in args[:6]:
        load.wait()
    for i, ref in enumerate((press, source, coupling)):
        pack[0, pl.ds(8 * i, 8), :] = ref[:, 0:128].T[0:8]
        pack[1, pl.ds(8 * i, 8), :] = ref[:, 128:256].T[120:128]
    for j in range(2):
        lanes = slice(128 * j, 128 * j + 128)
        pack[j, pl.ds(24, 8), :] = jnp.concatenate(
            [lower[:, lanes], mask[:, lanes].astype(F32), jnp.zeros((6, 128), F32)], axis=0
        )
    gain_m = binv[127:128, 0:1] * lower[...]
    first_row = binv[...].T[0:1]
    for j in range(2):
        lanes = slice(128 * j, 128 * j + 128)
        cs[j, 0:1, :] = gain_m[:, 0:128]
        cs[j, 1:2, :] = gain_m[:, 128:256]
        cs[j, 2:3, :] = lower[:, lanes]
        cs[j, 3:4, :] = mask[:, lanes].astype(F32)
        cs[j, 4:5, :] = first_row
    pl.semaphore_wait(barrier, N_ROLL + N_SIDE - 2)
    halo_copies = []
    for k in range(2):
        for j, d in ((0, N_SIDE - 1), (1, 1)):
            to = lax.rem(side + d, N_SIDE)
            s, dst = ((pack.at[j], halo.at[j]), (binv, bhalo.at[j]))[k]
            c = pltpu.make_async_remote_copy(
                src_ref=s, dst_ref=dst, send_sem=halo_ss.at[j, k], recv_sem=halo_rs.at[j, k],
                device_id={"side": to}, device_id_type=MESH,
            )
            c.start()
            halo_copies.append(c)
    send_roll(lambda to: cs.at[lax.rem(to, 2)], cr.at[me], 0)
    cr[me] = cs[half]
    bhi, blo = split(binv[...])
    b3[:, 0:128] = bhi
    b3[:, 128:256] = bhi
    b3[:, 256:384] = blo
    halo_copies[0].wait()
    halo_copies[1].wait()
    has_right = side < N_SIDE - 1
    has_left = side > 0
    is_right = lane_b < 64
    valid = jnp.logical_or(
        jnp.logical_and(is_right, has_right), jnp.logical_and(jnp.logical_not(is_right), has_left)
    )
    ext = []
    for i in range(3):
        tall = jnp.concatenate(
            [halo[0, pl.ds(8 * i, 8), :], jnp.zeros((112, 128), F32), halo[1, pl.ds(8 * i, 8), :]],
            axis=0,
        )
        ext.append(jnp.where(valid, tall.T, 0.0))
    row_right = is_right[0:1]
    row_valid = valid[0:1]
    lower_e = jnp.where(row_valid, jnp.where(row_right, halo[0, 24:25, :], halo[1, 24:25, :]), 0.0)
    mask_e = jnp.where(row_right, halo[0, 25:26, :], halo[1, 25:26, :]) > 0.5
    halo_copies[2].wait()
    halo_copies[3].wait()
    rhi, rlo = split(bhalo[0])
    lhi, llo = split(bhalo[1])
    for i, part in enumerate((rhi, lhi, rhi, lhi, rlo, llo)):
        be3[:, pl.ds(128 * i, 128)] = part
    first_e = jnp.where(is_right, bhalo[0, :, 0:1], bhalo[1, :, 0:1])
    first = binv[:, 0:1]
    lower_w = jnp.concatenate([lower[...], lower_e], axis=1)
    mask_w = jnp.concatenate([mask[...].astype(F32), mask_e.astype(F32)], axis=1) > 0.5
    first_w = jnp.concatenate([jnp.broadcast_to(first, (ROWS, COLS)), first_e], axis=1)
    source_w = jnp.concatenate([source[...], ext[1]], axis=1)
    coupling_w = jnp.concatenate([coupling[...], ext[2]], axis=1)
    field = jnp.concatenate([press[...], ext[0]], axis=1)
    outs0[3:4, :] = first_e[127:128] * lower_e

    for sweep in range(SWEEPS - 1):
        rhs = source_w + coupling_w * (pltpu.roll(field, 1, 1) + pltpu.roll(field, 383, 1))
        hi, lo = split(rhs[:, :256])
        stack = jnp.concatenate([hi, lo, hi], axis=0)
        he = rhs[:, 256:]
        hr, lr = split(jnp.where(is_right, he, 0.0))
        hl, ll = split(jnp.where(is_right, 0.0, he))
        stack_e = jnp.concatenate([hr, hl, lr, ll, hr, hl], axis=0)
        tail = mm(b3[112:128, :], stack)
        tail_e = mm(be3[112:128, :], stack_e)
        out = outs0 if sweep == 0 else outs.at[sweep - 1]
        for i in range(3):
            row = tail_e[15:16] if i == 2 else tail[15:16, 128 * i : 128 * i + 128]
            out[i : i + 1, :] = row
        into = recv0 if sweep == 0 else recv.at[sweep - 1]
        send_roll(lambda to: out, into.at[me], 1 + sweep)
        local = jnp.concatenate([mm(b3[...], stack), mm(be3[...], stack_e)], axis=1)
        if sweep == 0:
            i = lax.broadcasted_iota(jnp.int32, (16, COLS), 0)
            q = 16 * side + i
            lane = lax.broadcasted_iota(jnp.int32, (16, COLS), 1)
            reach = min(FFT_X, FFT_Y) / 16.0
            scale = 0.4 * reach / (float(FFT_X) * float(FFT_Y))
            for part in range(2):
                if part == 0:
                    u_first = 128 * jnp.where(q <= 64, q, q - 64)
                    single = jnp.logical_and(me == 0, jnp.logical_or(q == 0, q == 64))
                    weight = jnp.where(single, scale, 2.0 * scale)
                else:
                    u_first = 64 + 128 * jnp.where(q < 64, q, q - 64)
                    weight = jnp.full((16, COLS), 2.0 * scale, F32)
                u = jnp.where(me == 0, u_first, me + 128 * q)
                fu = jnp.minimum(u, FFT_X - u).astype(F32) / FFT_X
                fu2 = fu * fu
                for v1 in range(CLASSES):
                    v = v1 + 16 * lane
                    fv = jnp.minimum(v, FFT_Y - v).astype(F32) / FFT_Y
                    w = weight if v1 in (0, 8) else 2.0 * weight
                    kern[part, pl.ds(16 * v1, 16), :] = w / (
                        1.0 + reach * jnp.sqrt(fu2 + fv * fv)
                    )
            settle(cr.at[rest], cr.at[rest], 0)
            gfull[:, 0:2, :] = cr[:, 0:2, :]
        if sweep == 1:
            loads[4].wait()
            loads[5].wait()
            mrow = maint[0] * slant[0:1, :] + maint[1] * slant[1:2, :]
            hi, lo = split(mrow)
            m3[:, 0:256] = hi
            m3[:, 256:512] = hi
            m3[:, 512:768] = lo
            bt[...] = jnp.zeros_like(bt)
            for a in range(N_ROLL):
                bt[a : a + 1, :] = cr[a, 4:5, :]
                gsel[a] = jnp.where(half == 0, cr[a, 0:1, :], cr[a, 1:2, :])
        if sweep == 2:
            mrow = maint[0] * slant[0:1, :] + maint[1] * slant[1:2, :]
            hi, lo = split(mrow.T)
            mt3[:, 0:256] = hi
            mt3[:, 256:512] = hi
            mt3[:, 512:768] = lo
            btt[...] = bt[...].T.reshape(32, 4, 128)
            mine = btt[group]
            for a in range(N_ROLL):
                bx[a] = jnp.broadcast_to(mine[:, a : a + 1], (4, 128))
        settle(into.at[rest], into.at[rest], 1 + sweep)
        if sweep == 0:
            gfull[:, 2:3, :] = recv0[:, 3:4, :]

        def advance(k8, c):
            for j in range(8):
                k = 8 * k8 + j
                carry_buf[k] = c
                flow = recv0[k, 0:3] if sweep == 0 else recv[sweep - 1, k]
                c = flow + gfull[k] * c
            return c

        lax.fori_loop(0, N_ROLL // 8, advance, jnp.zeros((3, 128), F32))
        mine = carry_buf[me]
        carry = jnp.concatenate([mine[0:1], mine[1:2], mine[2:3]], axis=1)
        solved = local + first_w * (lower_w * carry)
        field = jnp.where(mask_w, jnp.maximum(solved, 0.0), solved)

    rhs = source_w + coupling_w * (pltpu.roll(field, 1, 1) + pltpu.roll(field, 383, 1))
    hi, lo = split(rhs[:, :256])
    local = mm(b3[...], jnp.concatenate([hi, lo, hi], axis=0))
    for h in range(2):
        tile = local[:, 128 * h : 128 * h + 128]
        p1s[pl.ds(32 * h, 32), 0:4, :] = tile.reshape(32, 4, 128)
        p1s[pl.ds(32 * h, 32), 4:5, :] = jnp.broadcast_to(tile[127:128].reshape(1, 1, 128), (32, 1, 128))
    send_roll(lambda to: p1s.at[place(to)], p1r.at[me], 4)
    p1r[me] = p1s[place(me)]
    loc4[...] = local
    loads[0].wait()
    settle(p1s.at[rest], p1r.at[rest], 4)

    def finish(k8, c):
        for j in range(8):
            k = 8 * k8 + j
            carry4[k] = c
            sol = p1r[k, 0:4, :] + bx[k] * (cr[k, 2:3, :] * c)
            qf[k] = jnp.where(cr[k, 3:4, :] > 0.5, jnp.maximum(sol, 0.0), sol)
            c = p1r[k, 4:5, :] + gsel[k] * c
        return c

    lax.fori_loop(0, N_ROLL // 8, finish, jnp.zeros((1, 128), F32))
    hi, lo = split(qf[...].reshape(256, 128))
    q3[0:256] = hi
    q3[256:512] = lo
    q3[512:768] = hi
    p2s[...] = mm(w3[...], q3[...]).reshape(64, 8, 128)

    send_roll(lambda to: p2s.at[to], p2r.at[place(me)], 5)
    push(carry4.at[other], partner, 6, {"roll": other})
    p2r[place(me)] = p2s[me]
    settle(carry4.at[0], partner, 6)
    for h in range(2):
        lanes = slice(128 * h, 128 * h + 128)
        carry = jnp.where(half == h, carry4[me], partner[...])
        sol = loc4[:, lanes] + binv[:, 0:1] * (lower[:, lanes] * carry)
        newp[:, lanes] = jnp.where(mask[:, lanes] == 1, jnp.maximum(sol, 0.0), sol)
    save_p = pltpu.make_async_copy(newp, newp_h, out_sem.at[0])
    save_p.start()
    settle(p2s.at[rest], p2r.at[rest], 5)
    for h in range(2):
        hi, lo = split(p2r[pl.ds(32 * h, 32)].reshape(256, 128))
        lanes = slice(128 * h, 128 * h + 128)
        x3[0:256, lanes] = hi
        x3[256:512, lanes] = lo
        x3[512:768, lanes] = hi

    for part in range(2):
        us[part] = mm(m3[128 * part : 128 * part + 128, :], x3[...]).reshape(8, 16, 256)
        send_side(lambda to: us.at[part, to], yb.at[part, side], 7 + part)
        yb[part, side] = us[part, side]
    loads[2].wait()
    loads[3].wait()
    loads[6].wait()

    cosines = [[math.cos(math.pi * s * v / 8.0) for v in range(9)] for s in range(8)]
    sines = [[math.sin(math.pi * s * v / 8.0) for v in range(9)] for s in range(8)]

    def put(v1, lanes, re, im):
        at = 16 * v1
        for which, value in ((0, re), (256, im)):
            hi, lo = split(value)
            zs[pl.ds(at, 16), pl.ds(which + lanes, 128)] = hi
            zs[pl.ds(at, 16), pl.ds(512 + which + lanes, 128)] = lo
            zs[pl.ds(at, 16), pl.ds(1024 + which + lanes, 128)] = hi

    for part in range(2):
        settle(us.at[part, rest_side], yb.at[part, rest_side], 7 + part)
        for lanes in (0, 128):
            x = [yb[part, s, :, pl.ds(lanes, 128)] for s in range(8)]
            for v in range(5):
                er = combine([(cosines[s][v], x[s]) for s in (0, 2, 4, 6)])
                orr = combine([(cosines[s][v], x[s]) for s in (1, 3, 5, 7)])
                ei = combine([(-sines[s][v], x[s]) for s in (0, 2, 4, 6)])
                oi = combine([(-sines[s][v], x[s]) for s in (1, 3, 5, 7)])
                zero = jnp.zeros((16, 128), F32)
                ei = zero if ei is None else ei
                oi = zero if oi is None else oi
                orr = zero if orr is None else orr
                todo = [(v, er + orr, ei + oi)]
                if v < 4:
                    todo.append((8 - v, er - orr, oi - ei))
                for v1, yr, yi in todo:
                    c = twid[0, v1 : v1 + 1, lanes : lanes + 128]
                    s = twid[1, v1 : v1 + 1, lanes : lanes + 128]
                    put(v1, lanes, yr * c + yi * s, yi * c - yr * s)
        spec = mm(zs[...], d3[...])
        for v1 in range(CLASSES):
            at = 16 * v1
            for lanes in (0, 128):
                k = kern[part, pl.ds(at, 16), pl.ds(lanes, 128)]
                put(
                    v1, lanes,
                    spec[at : at + 16, lanes : lanes + 128] * k,
                    spec[at : at + 16, 256 + lanes : 384 + lanes] * k,
                )
        back = mm(zs[...], dt3[...])
        for lanes in (0, 128):
            yr, yi = [], []
            for v1 in range(CLASSES):
                at = 16 * v1
                zr = back[at : at + 16, lanes : lanes + 128]
                zi = back[at : at + 16, 256 + lanes : 384 + lanes]
                c = twid[0, v1 : v1 + 1, lanes : lanes + 128]
                s = twid[1, v1 : v1 + 1, lanes : lanes + 128]
                yr.append(zr * c - zi * s)
                yi.append(zr * s + zi * c)
            plus_r = [yr[v] + yr[8 - v] for v in range(4)] + [yr[4]]
            plus_i = [yi[v] + yi[8 - v] for v in range(4)] + [yi[4]]
            less_r = [yr[v] - yr[8 - v] for v in range(4)] + [yr[4]]
            less_i = [yi[v] - yi[8 - v] for v in range(4)] + [yi[4]]
            h = lanes // 128
            for s in range(8):
                re, im = (plus_r, less_i) if s % 2 == 0 else (less_r, plus_i)
                ob[h, part, s] = combine(
                    [(cosines[s][v], re[v]) for v in range(5)]
                    + [(-sines[s][v], im[v]) for v in range(5)]
                )
            send_side(lambda to: ob.at[h, part, to], ub.at[h, part, side], 9 + 2 * h + part)
            ub[h, part, side] = ob[h, part, side]

    for h in range(2):
        for part in range(2):
            settle(ob.at[h, part, rest_side], ub.at[h, part, rest_side], 9 + 2 * h + part)
        hi, lo = split(ub[h].reshape(256, 128))
        v3[0:256] = hi
        v3[256:512] = lo
        v3[512:768] = hi
        p5s[pl.ds(32 * h, 32)] = mm(mt3[...], v3[0:768]).reshape(32, 8, 128)

        def body(i, _):
            to = far(2 * i + 1, along_x, along_z, h)
            push(p5s.at[place(to)], p5r.at[me], 13, {"roll": to})
            return 0

        lax.fori_loop(0, 31, body, 0)

        @pl.when(half != h)
        def _():
            push(p5s.at[place(other)], p5r.at[me], 13, {"roll": other})

    p5r[me] = p5s[place(me)]
    loads[1].wait()
    settle(p5s.at[rest], p5r.at[rest], 13)
    hi, lo = split(p5r[...].reshape(512, 128))
    v3[0:512] = hi
    v3[512:1024] = lo
    v3[1024:1536] = hi
    p6s[...] = mm(wt3[...], v3[...]).reshape(64, 4, 128)

    send_roll(lambda to: p6s.at[to], p6r.at[place(me)], 14)
    p6r[place(me)] = p6s[me]
    row_pos = (me * ROWS + lax.broadcasted_iota(jnp.int32, (ROWS, COLS), 0)).astype(F32)
    col_pos = (side * COLS + lax.broadcasted_iota(jnp.int32, (ROWS, COLS), 1)).astype(F32)
    across = 4.0 * (row_pos + 0.5) / (ROWS * N_ROLL) - 2.5
    transverse = 4.0 * (col_pos + 0.5) / (COLS * N_SIDE) - 2.0
    ground = offset[0] + 0.5 * across * across + 0.5 * transverse * transverse
    args[6].wait()
    ripple = ROUGH_STEP * rough[...].astype(F32)
    settle(p6s.at[rest], p6r.at[rest], 14)
    for h in range(2):
        lanes = slice(128 * h, 128 * h + 128)
        bend = p6r[pl.ds(32 * h, 32)].reshape(128, 128)
        film[:, lanes] = ground[:, lanes] + bend - ripple[:, lanes]
    save_f = pltpu.make_async_copy(film, film_h, out_sem.at[1])
    save_f.start()
    save_p.wait()
    save_f.wait()


def per_device(pressure, source, coupling, binv, lower, mask, rough, offset):
    consts = [jnp.asarray(t) for t in tables()]
    hbm = pl.BlockSpec(memory_space=pl.ANY)
    f = lambda *shape: pltpu.VMEM(shape, F32)
    b = lambda *shape: pltpu.VMEM(shape, BF16)
    i32 = lambda *shape: pltpu.VMEM(shape, jnp.int32)
    scratch = [
        f(128, 256), f(128, 256), f(128, 256), f(128, 128), f(1, 256), i32(1, 256), i32(128, 256),
        f(128, 256), f(128, 256),
        b(512, 768), b(256, 1536), b(1536, 512), b(1536, 512),
        f(2, 256, 256), f(2, 256), f(2, 16, 256),
        f(2, 32, 128), f(2, 32, 128), f(2, 128, 128),
        f(2, 5, 128), f(64, 5, 128), f(4, 128), f(2, 3, 128), f(64, 4, 128), f(2, 64, 3, 128),
        f(64, 3, 128), f(64, 3, 128), f(64, 1, 128), f(128, 128), f(32, 4, 128), f(64, 4, 128),
        f(64, 1, 128), f(1, 128),
        b(128, 384), b(128, 768), f(128, 256),
        f(2, 144, 256), b(256, 768), b(256, 768),
        f(64, 5, 128), f(64, 5, 128), f(64, 4, 128), b(768, 128), f(64, 8, 128), f(64, 8, 128),
        b(768, 256), f(2, 8, 16, 256), f(2, 8, 16, 256), b(144, 1536), f(2, 2, 8, 16, 128),
        f(2, 2, 8, 16, 128), f(64, 8, 128), f(64, 8, 128), b(1536, 128), f(64, 4, 128),
        f(64, 4, 128),
        pltpu.SemaphoreType.DMA((7,)), pltpu.SemaphoreType.DMA((7,)), pltpu.SemaphoreType.DMA((2,)),
        pltpu.SemaphoreType.DMA((2, 2)), pltpu.SemaphoreType.DMA((2, 2)),
        pltpu.SemaphoreType.DMA((15,)), pltpu.SemaphoreType.DMA((15,)),
    ]
    out = jax.ShapeDtypeStruct((ROWS, COLS), F32)
    return pl.pallas_call(
        main_kernel,
        out_shape=(out, out),
        in_specs=[hbm] * 7 + [pl.BlockSpec(memory_space=pltpu.SMEM)] + [hbm] * 7,
        out_specs=(hbm, hbm),
        scratch_shapes=scratch,
        compiler_params=pltpu.CompilerParams(
            collective_id=0, has_side_effects=True, vmem_limit_bytes=56 * 1024 * 1024
        ),
    )(pressure, source, coupling, binv, lower, mask, rough, offset, *consts)


def solution(mesh):
    spec = P("roll", "side")
    return jax.shard_map(
        per_device,
        mesh=mesh,
        in_specs=(spec,) * 7 + (P(),),
        out_specs=(spec, spec),
        check_vma=False,
    )
```

```python
import functools
import math

import jax
import jax.numpy as jnp
import ml_dtypes
import numpy as np
from jax import lax
from jax.experimental import pallas as pl
from jax.experimental.pallas import tpu as pltpu
from jax.sharding import PartitionSpec as P

SWEEPS = 4
ROUGH_STEP = 0.05
MESH = pl.DeviceIdType.MESH
F32 = jnp.float32
BF16 = jnp.bfloat16

N_ROLL, N_SIDE = 64, 8
ROWS, COLS = 128, 256
FFT_X, FFT_Y = 2 * N_ROLL * ROWS, 2 * N_SIDE * COLS
CLASSES = N_SIDE + 1


def split_np(x):
    x = x.astype(np.float32)
    hi = x.astype(ml_dtypes.bfloat16)
    lo = (x - hi.astype(np.float32)).astype(ml_dtypes.bfloat16)
    return hi, lo


def wide_np(x, axis):
    hi, lo = split_np(x)
    return np.concatenate([hi, hi, lo], axis=axis)


def turns(ints, length):
    return 2.0 * np.pi * (ints % length).astype(np.float64) / length


@functools.lru_cache(None)
def tables():
    a = np.arange(N_ROLL)
    ang = turns(a[:, None] * a[None, :], 2 * N_ROLL)
    sect = np.stack([np.cos(ang), -np.sin(ang)], axis=1)
    sect[0, 1] = np.where(a % 2 == 0, 1.0, -1.0)
    sect = np.einsum("uca,ij->uciaj", sect, np.eye(4)).reshape(8 * N_ROLL, 4 * N_ROLL)
    c = np.arange(COLS)
    ang = turns(c[:, None] * c[None, :], COLS)
    dcos, dsin = np.cos(ang), np.sin(ang)
    dft = np.block([[dcos, -dsin], [dsin, dcos]])
    v1 = np.arange(16)
    ang = turns(v1[:, None] * c[None, :], FFT_Y)
    twiddle = np.stack([np.cos(ang), np.sin(ang)]).astype(np.float32)
    q = np.arange(ROWS).reshape(N_SIDE, 16)
    t = np.arange(ROWS).reshape(32, 4)
    ang = turns(q[:, :, None, None] * t[None, None], ROWS)
    cb, sb = np.cos(ang), np.sin(ang)
    main = np.zeros((2, 2, 2, N_SIDE, 16, 32, 2, 4))
    main[1, 0, 0, :, :, :, 0], main[1, 0, 0, :, :, :, 1] = cb, sb
    main[1, 0, 1, :, :, :, 0], main[1, 0, 1, :, :, :, 1] = -sb, cb
    main[1, 1, 0, :, :, :, 0], main[1, 1, 0, :, :, :, 1] = -sb, cb
    main[1, 1, 1, :, :, :, 0], main[1, 1, 1, :, :, :, 1] = -cb, -sb
    even = np.where(q <= 64, q, q - 64)
    ang = turns(even[:, :, None, None] * t[None, None], ROWS)
    main[0, 0, 0, :, :, :, 0] = np.where((q <= 64)[:, :, None, None], np.cos(ang), np.sin(ang))
    odd = 64 + 128 * np.where(q < 64, q, q - 64)
    ang = turns(odd[:, :, None, None] * t[None, None], FFT_X)
    main[0, 0, 1, :, :, :, 1] = np.where((q < 64)[:, :, None, None], np.cos(ang), np.sin(ang))
    main = main.reshape(2, 2, 256, 256).astype(np.float32)
    cols_t = np.broadcast_to(t[:, None, :], (32, 2, 4)).reshape(256)
    ang = turns(a[:, None] * cols_t[None, :], FFT_X)
    slant = np.stack([np.cos(ang), np.sin(ang)], axis=1).astype(np.float32)
    return (
        wide_np(sect, 1),
        wide_np(sect.T, 1),
        wide_np(dft, 0),
        wide_np(dft.T, 0),
        main,
        slant,
        twiddle,
    )


def split(x):
    hi = x.astype(BF16)
    return hi, (x - hi.astype(F32)).astype(BF16)


def mm(a, b):
    return jnp.dot(a, b, preferred_element_type=F32)


def place(device):
    return lax.rem(device, 2) * 32 + lax.div(device, 2)


def combine(terms):
    total = None
    for coef, value in terms:
        if abs(coef) < 1e-12:
            continue
        if abs(coef - 1.0) < 1e-12:
            total = value if total is None else total + value
        elif abs(coef + 1.0) < 1e-12:
            total = -value if total is None else total - value
        else:
            total = coef * value if total is None else total + coef * value
    return total


def far(i, x, z, c):
    m, n = lax.div(i, 8), lax.div(lax.rem(i, 8), 2)
    dz = 4 + lax.div(m + 1, 2) * (1 - 2 * lax.rem(m, 2))
    dx = 2 + lax.div(n + 1, 2) * (1 - 2 * lax.rem(n, 2))
    return (
        lax.rem(x + dx, 4) * 16 + lax.rem(z + dz, 8) * 2 + lax.rem(c + 1 - lax.rem(i, 2), 2)
    )


def main_kernel(
    press_h, source_h, coupling_h, binv_h, lower_h, mask_h, rough_h, offset,
    w3_h, wt3_h, d3_h, dt3_h, main_h, slant_h, twid_h,
    newp, film,
    press, source, coupling, binv, lower, mask, rough,
    w3, wt3, d3, dt3, maint, slant, twid,
    pack, halo, bhalo,
    cs, cr, outs0, outs, recv0, recv, gfull, gpre, gall, cgroup, carry_buf, gsel, gsel_pre, gsel_all, bt, btt, bx, carry4, partner,
    b3, be3, loc4,
    kern, m3, mt3,
    p1s, p1r, qf, q3, p2s, p2r, x3, us, yb, zs, ob, ub, p5s, p5r, v3, p6s, p6r,
    const_sem, arg_sem, known, halo_ss, halo_rs, ss, rs,
):
    me = lax.axis_index("roll")
    side = lax.axis_index("side")
    along_x, along_z, half = lax.div(me, 16), lax.rem(lax.div(me, 2), 8), lax.rem(me, 2)
    group = lax.div(me, 2)
    other = me + 1 - 2 * half
    barrier = pltpu.get_barrier_semaphore()

    def greet(sem, where):
        pl.semaphore_signal(sem, inc=1, device_id=where, device_id_type=MESH)

    def plane(i):
        n = lax.div(i, 2)
        dx = 2 + lax.div(n + 1, 2) * (1 - 2 * lax.rem(n, 2))
        core = lax.rem(half + 1 - lax.rem(i, 2), 2)
        return lax.rem(along_x + dx, 4) * 16 + along_z * 2 + core

    for d in (4, 3, 5, 2, 6, 1, 7):
        greet(barrier, {"roll": along_x * 16 + lax.rem(along_z + d, 8) * 2 + half})
        greet(barrier, {"side": lax.rem(side + d, N_SIDE)})
    for i in range(7):
        greet(barrier, {"roll": plane(i)})

    variant = jnp.minimum(me, 1)
    loads = [
        pltpu.make_async_copy(s, d, const_sem.at[i])
        for i, (s, d) in enumerate(
            [
                (w3_h, w3), (wt3_h, wt3), (d3_h, d3), (dt3_h, dt3),
                (main_h.at[variant], maint), (slant_h.at[me], slant), (twid_h, twid),
            ]
        )
    ]
    args = [
        pltpu.make_async_copy(s, d, arg_sem.at[i])
        for i, (s, d) in enumerate(
            [
                (press_h, press), (source_h, source), (coupling_h, coupling), (binv_h, binv),
                (lower_h, lower), (mask_h, mask), (rough_h, rough),
            ]
        )
    ]
    for load in args:
        load.start()
    for load in loads:
        load.start()

    def push(src, dst, phase, where):
        pltpu.make_async_remote_copy(
            src_ref=src, dst_ref=dst, send_sem=ss.at[phase], recv_sem=rs.at[phase],
            device_id=where, device_id_type=MESH,
        ).start()

    def send_roll(src_at, dst, phase):
        def body(i, _):
            to = far(i, along_x, along_z, half)
            push(src_at(to), dst, phase, {"roll": to})
            return 0

        lax.fori_loop(0, N_ROLL - 1, body, 0)

    def send_side(src_at, dst, phase):
        for d in (4, 3, 5, 2, 6, 1, 7):
            to = lax.rem(side + d, N_SIDE)
            push(src_at(to), dst, phase, {"side": to})

    def settle(src, dst, phase):
        pltpu.make_async_remote_copy(
            src_ref=src, dst_ref=dst, send_sem=ss.at[phase], recv_sem=rs.at[phase],
            device_id={"roll": other}, device_id_type=MESH,
        ).wait()

    rest = pl.ds(0, N_ROLL - 1)
    rest_side = pl.ds(0, N_SIDE - 1)

    lane_b = lax.broadcasted_iota(jnp.int32, (ROWS, 128), 1)
    for load in args[:6]:
        load.wait()
    for i, ref in enumerate((press, source, coupling)):
        pack[0, pl.ds(8 * i, 8), :] = ref[:, 0:128].T[0:8]
        pack[1, pl.ds(8 * i, 8), :] = ref[:, 128:256].T[120:128]
    for j in range(2):
        lanes = slice(128 * j, 128 * j + 128)
        pack[j, pl.ds(24, 8), :] = jnp.concatenate(
            [lower[:, lanes], mask[:, lanes].astype(F32), jnp.zeros((6, 128), F32)], axis=0
        )
    gain_m = binv[127:128, 0:1] * lower[...]
    first_row = binv[...].T[0:1]
    for j in range(2):
        lanes = slice(128 * j, 128 * j + 128)
        cs[j, 0:1, :] = gain_m[:, 0:128]
        cs[j, 1:2, :] = gain_m[:, 128:256]
        cs[j, 2:3, :] = lower[:, lanes]
        cs[j, 3:4, :] = mask[:, lanes].astype(F32)
        cs[j, 4:5, :] = first_row
    pl.semaphore_wait(barrier, 21)
    halo_copies = []
    for k in range(2):
        for j, d in ((0, N_SIDE - 1), (1, 1)):
            to = lax.rem(side + d, N_SIDE)
            s, dst = ((pack.at[j], halo.at[j]), (binv, bhalo.at[j]))[k]
            c = pltpu.make_async_remote_copy(
                src_ref=s, dst_ref=dst, send_sem=halo_ss.at[j, k], recv_sem=halo_rs.at[j, k],
                device_id={"side": to}, device_id_type=MESH,
            )
            c.start()
            halo_copies.append(c)
    for i in range(7):
        greet(known, {"roll": plane(i)})
    cr[me] = cs[half]
    bhi, blo = split(binv[...])
    b3[:, 0:128] = bhi
    b3[:, 128:256] = bhi
    b3[:, 256:384] = blo
    pl.semaphore_wait(known, 7)
    send_roll(lambda to: cs.at[lax.rem(to, 2)], cr.at[me], 0)
    halo_copies[0].wait()
    halo_copies[1].wait()
    has_right = side < N_SIDE - 1
    has_left = side > 0
    is_right = lane_b < 64
    valid = jnp.logical_or(
        jnp.logical_and(is_right, has_right), jnp.logical_and(jnp.logical_not(is_right), has_left)
    )
    ext = []
    for i in range(3):
        tall = jnp.concatenate(
            [halo[0, pl.ds(8 * i, 8), :], jnp.zeros((112, 128), F32), halo[1, pl.ds(8 * i, 8), :]],
            axis=0,
        )
        ext.append(jnp.where(valid, tall.T, 0.0))
    row_right = is_right[0:1]
    row_valid = valid[0:1]
    lower_e = jnp.where(row_valid, jnp.where(row_right, halo[0, 24:25, :], halo[1, 24:25, :]), 0.0)
    mask_e = jnp.where(row_right, halo[0, 25:26, :], halo[1, 25:26, :]) > 0.5
    first = binv[:, 0:1]
    lower_w = jnp.concatenate([lower[...], lower_e], axis=1)
    mask_w = jnp.concatenate([mask[...].astype(F32), mask_e.astype(F32)], axis=1) > 0.5
    source_w = jnp.concatenate([source[...], ext[1]], axis=1)
    coupling_w = jnp.concatenate([coupling[...], ext[2]], axis=1)
    field = jnp.concatenate([press[...], ext[0]], axis=1)

    for sweep in range(SWEEPS - 1):
        rhs = source_w + coupling_w * (pltpu.roll(field, 1, 1) + pltpu.roll(field, 383, 1))
        hi, lo = split(rhs[:, :256])
        stack = jnp.concatenate([hi, lo, hi], axis=0)
        he = rhs[:, 256:]
        hr, lr = split(jnp.where(is_right, he, 0.0))
        hl, ll = split(jnp.where(is_right, 0.0, he))
        stack_e = jnp.concatenate([hr, hl, lr, ll, hr, hl], axis=0)
        tail = mm(b3[112:128, :], stack)
        if sweep == 0:
            halo_copies[2].wait()
            halo_copies[3].wait()
            rhi, rlo = split(bhalo[0])
            lhi, llo = split(bhalo[1])
            for i, part in enumerate((rhi, lhi, rhi, lhi, rlo, llo)):
                be3[:, pl.ds(128 * i, 128)] = part
            first_e = jnp.where(is_right, bhalo[0, :, 0:1], bhalo[1, :, 0:1])
            first_w = jnp.concatenate([jnp.broadcast_to(first, (ROWS, COLS)), first_e], axis=1)
            outs0[3:4, :] = first_e[127:128] * lower_e
        tail_e = mm(be3[112:128, :], stack_e)
        out = outs0 if sweep == 0 else outs.at[sweep - 1]
        for i in range(3):
            row = tail_e[15:16] if i == 2 else tail[15:16, 128 * i : 128 * i + 128]
            out[i : i + 1, :] = row
        into = recv0 if sweep == 0 else recv.at[sweep - 1]
        send_roll(lambda to: out, into.at[me], 1 + sweep)
        local = jnp.concatenate([mm(b3[...], stack), mm(be3[...], stack_e)], axis=1)
        if sweep == 0:
            i = lax.broadcasted_iota(jnp.int32, (16, COLS), 0)
            q = 16 * side + i
            lane = lax.broadcasted_iota(jnp.int32, (16, COLS), 1)
            reach = min(FFT_X, FFT_Y) / 16.0
            scale = 0.4 * reach / (float(FFT_X) * float(FFT_Y))
            for part in range(2):
                if part == 0:
                    u_first = 128 * jnp.where(q <= 64, q, q - 64)
                    single = jnp.logical_and(me == 0, jnp.logical_or(q == 0, q == 64))
                    weight = jnp.where(single, scale, 2.0 * scale)
                else:
                    u_first = 64 + 128 * jnp.where(q < 64, q, q - 64)
                    weight = jnp.full((16, COLS), 2.0 * scale, F32)
                u = jnp.where(me == 0, u_first, me + 128 * q)
                fu = jnp.minimum(u, FFT_X - u).astype(F32) / FFT_X
                fu2 = fu * fu
                for v1 in range(CLASSES):
                    v = v1 + 16 * lane
                    fv = jnp.minimum(v, FFT_Y - v).astype(F32) / FFT_Y
                    w = weight if v1 in (0, 8) else 2.0 * weight
                    kern[part, pl.ds(16 * v1, 16), :] = w / (
                        1.0 + reach * jnp.sqrt(fu2 + fv * fv)
                    )
            settle(cr.at[rest], cr.at[rest], 0)
            gfull[:, 0:2, :] = cr[:, 0:2, :]
        if sweep == 1:
            loads[4].wait()
            loads[5].wait()
            mrow = maint[0] * slant[0:1, :] + maint[1] * slant[1:2, :]
            hi, lo = split(mrow)
            m3[:, 0:256] = hi
            m3[:, 256:512] = hi
            m3[:, 512:768] = lo
            bt[...] = jnp.zeros_like(bt)
            for a in range(N_ROLL):
                bt[a : a + 1, :] = cr[a, 4:5, :]
                gain = jnp.where(half == 0, cr[a, 0:1, :], cr[a, 1:2, :])
                gsel[a] = gain
                gsel_pre[a] = jnp.ones((1, 128), F32) if a % 8 == 0 else product
                product = gain if a % 8 == 0 else product * gain
                if a % 8 == 7:
                    gsel_all[a // 8] = product
        if sweep == 2:
            mrow = maint[0] * slant[0:1, :] + maint[1] * slant[1:2, :]
            hi, lo = split(mrow.T)
            mt3[:, 0:256] = hi
            mt3[:, 256:512] = hi
            mt3[:, 512:768] = lo
            btt[...] = bt[...].T.reshape(32, 4, 128)
            mine = btt[group]
            for a in range(N_ROLL):
                bx[a] = jnp.broadcast_to(mine[:, a : a + 1], (4, 128))
        settle(into.at[rest], into.at[rest], 1 + sweep)
        if sweep == 0:
            gfull[:, 2:3, :] = recv0[:, 3:4, :]

        totals = []
        for g in range(8):
            c = flow = None
            for j in range(8):
                k = 8 * g + j
                flow = recv0[k, 0:3] if sweep == 0 else recv[sweep - 1, k]
                gain = gfull[k]
                carry_buf[k] = jnp.zeros((3, 128), F32) if c is None else c
                c = flow if c is None else flow + gain * c
                if sweep == 0:
                    gpre[k] = jnp.ones((3, 128), F32) if j == 0 else product
                    product = gain if j == 0 else product * gain
            if sweep == 0:
                gall[g] = product
            totals.append(c)
        c = jnp.zeros((3, 128), F32)
        for g in range(8):
            cgroup[g] = c
            c = totals[g] + gall[g] * c
        mine = carry_buf[me] + gpre[me] * cgroup[lax.div(me, 8)]
        carry = jnp.concatenate([mine[0:1], mine[1:2], mine[2:3]], axis=1)
        solved = local + first_w * (lower_w * carry)
        field = jnp.where(mask_w, jnp.maximum(solved, 0.0), solved)

    rhs = source_w + coupling_w * (pltpu.roll(field, 1, 1) + pltpu.roll(field, 383, 1))
    hi, lo = split(rhs[:, :256])
    local = mm(b3[...], jnp.concatenate([hi, lo, hi], axis=0))
    for h in range(2):
        tile = local[:, 128 * h : 128 * h + 128]
        p1s[pl.ds(32 * h, 32), 0:4, :] = tile.reshape(32, 4, 128)
        p1s[pl.ds(32 * h, 32), 4:5, :] = jnp.broadcast_to(tile[127:128].reshape(1, 1, 128), (32, 1, 128))
    send_roll(lambda to: p1s.at[place(to)], p1r.at[me], 4)
    p1r[me] = p1s[place(me)]
    loc4[...] = local
    loads[0].wait()
    settle(p1s.at[rest], p1r.at[rest], 4)

    inner, totals = [], []
    for g in range(8):
        c = None
        for j in range(8):
            k = 8 * g + j
            inner.append(c)
            flow = p1r[k, 4:5, :]
            c = flow if c is None else flow + gsel[k] * c
        totals.append(c)
    c = jnp.zeros((1, 128), F32)
    for g in range(8):
        for j in range(8):
            k = 8 * g + j
            ck = c if j == 0 else inner[k] + gsel_pre[k] * c
            carry4[k] = ck
            sol = p1r[k, 0:4, :] + bx[k] * (cr[k, 2:3, :] * ck)
            qf[k] = jnp.where(cr[k, 3:4, :] > 0.5, jnp.maximum(sol, 0.0), sol)
        c = totals[g] + gsel_all[g] * c
    hi, lo = split(qf[...].reshape(256, 128))
    q3[0:256] = hi
    q3[256:512] = lo
    q3[512:768] = hi
    p2s[...] = mm(w3[...], q3[...]).reshape(64, 8, 128)

    send_roll(lambda to: p2s.at[to], p2r.at[place(me)], 5)
    push(carry4.at[other], partner, 6, {"roll": other})
    p2r[place(me)] = p2s[me]
    settle(carry4.at[0], partner, 6)
    for h in range(2):
        lanes = slice(128 * h, 128 * h + 128)
        carry = jnp.where(half == h, carry4[me], partner[...])
        sol = loc4[:, lanes] + binv[:, 0:1] * (lower[:, lanes] * carry)
        newp[:, lanes] = jnp.where(mask[:, lanes] == 1, jnp.maximum(sol, 0.0), sol)
    settle(p2s.at[rest], p2r.at[rest], 5)
    for h in range(2):
        hi, lo = split(p2r[pl.ds(32 * h, 32)].reshape(256, 128))
        lanes = slice(128 * h, 128 * h + 128)
        x3[0:256, lanes] = hi
        x3[256:512, lanes] = lo
        x3[512:768, lanes] = hi

    for part in range(2):
        us[part] = mm(m3[128 * part : 128 * part + 128, :], x3[...]).reshape(8, 16, 256)
        send_side(lambda to: us.at[part, to], yb.at[part, side], 7 + part)
        yb[part, side] = us[part, side]
    loads[2].wait()
    loads[3].wait()
    loads[6].wait()

    cosines = [[math.cos(math.pi * s * v / 8.0) for v in range(9)] for s in range(8)]
    sines = [[math.sin(math.pi * s * v / 8.0) for v in range(9)] for s in range(8)]

    def put(v1, lanes, re, im):
        at = 16 * v1
        for which, value in ((0, re), (256, im)):
            hi, lo = split(value)
            zs[pl.ds(at, 16), pl.ds(which + lanes, 128)] = hi
            zs[pl.ds(at, 16), pl.ds(512 + which + lanes, 128)] = lo
            zs[pl.ds(at, 16), pl.ds(1024 + which + lanes, 128)] = hi

    for part in range(2):
        settle(us.at[part, rest_side], yb.at[part, rest_side], 7 + part)
        for lanes in (0, 128):
            x = [yb[part, s, :, pl.ds(lanes, 128)] for s in range(8)]
            for v in range(5):
                er = combine([(cosines[s][v], x[s]) for s in (0, 2, 4, 6)])
                orr = combine([(cosines[s][v], x[s]) for s in (1, 3, 5, 7)])
                ei = combine([(-sines[s][v], x[s]) for s in (0, 2, 4, 6)])
                oi = combine([(-sines[s][v], x[s]) for s in (1, 3, 5, 7)])
                zero = jnp.zeros((16, 128), F32)
                ei = zero if ei is None else ei
                oi = zero if oi is None else oi
                orr = zero if orr is None else orr
                todo = [(v, er + orr, ei + oi)]
                if v < 4:
                    todo.append((8 - v, er - orr, oi - ei))
                for v1, yr, yi in todo:
                    c = twid[0, v1 : v1 + 1, lanes : lanes + 128]
                    s = twid[1, v1 : v1 + 1, lanes : lanes + 128]
                    put(v1, lanes, yr * c + yi * s, yi * c - yr * s)
        spec = mm(zs[...], d3[...])
        for v1 in range(CLASSES):
            at = 16 * v1
            for lanes in (0, 128):
                k = kern[part, pl.ds(at, 16), pl.ds(lanes, 128)]
                put(
                    v1, lanes,
                    spec[at : at + 16, lanes : lanes + 128] * k,
                    spec[at : at + 16, 256 + lanes : 384 + lanes] * k,
                )
        back = mm(zs[...], dt3[...])
        for lanes in (0, 128):
            yr, yi = [], []
            for v1 in range(CLASSES):
                at = 16 * v1
                zr = back[at : at + 16, lanes : lanes + 128]
                zi = back[at : at + 16, 256 + lanes : 384 + lanes]
                c = twid[0, v1 : v1 + 1, lanes : lanes + 128]
                s = twid[1, v1 : v1 + 1, lanes : lanes + 128]
                yr.append(zr * c - zi * s)
                yi.append(zr * s + zi * c)
            plus_r = [yr[v] + yr[8 - v] for v in range(4)] + [yr[4]]
            plus_i = [yi[v] + yi[8 - v] for v in range(4)] + [yi[4]]
            less_r = [yr[v] - yr[8 - v] for v in range(4)] + [yr[4]]
            less_i = [yi[v] - yi[8 - v] for v in range(4)] + [yi[4]]
            h = lanes // 128
            for s in range(8):
                re, im = (plus_r, less_i) if s % 2 == 0 else (less_r, plus_i)
                ob[h, part, s] = combine(
                    [(cosines[s][v], re[v]) for v in range(5)]
                    + [(-sines[s][v], im[v]) for v in range(5)]
                )
            send_side(lambda to: ob.at[h, part, to], ub.at[h, part, side], 9 + 2 * h + part)
            ub[h, part, side] = ob[h, part, side]

    for h in range(2):
        for part in range(2):
            settle(ob.at[h, part, rest_side], ub.at[h, part, rest_side], 9 + 2 * h + part)
        hi, lo = split(ub[h].reshape(256, 128))
        v3[0:256] = hi
        v3[256:512] = lo
        v3[512:768] = hi
        p5s[pl.ds(32 * h, 32)] = mm(mt3[...], v3[0:768]).reshape(32, 8, 128)

        def body(i, _):
            to = far(2 * i + 1, along_x, along_z, h)
            push(p5s.at[place(to)], p5r.at[me], 13, {"roll": to})
            return 0

        lax.fori_loop(0, 31, body, 0)

        @pl.when(half != h)
        def _():
            push(p5s.at[place(other)], p5r.at[me], 13, {"roll": other})

    p5r[me] = p5s[place(me)]
    loads[1].wait()
    settle(p5s.at[rest], p5r.at[rest], 13)
    hi, lo = split(p5r[...].reshape(512, 128))
    v3[0:512] = hi
    v3[512:1024] = lo
    v3[1024:1536] = hi
    p6s[...] = mm(wt3[...], v3[...]).reshape(64, 4, 128)

    send_roll(lambda to: p6s.at[to], p6r.at[place(me)], 14)
    p6r[place(me)] = p6s[me]
    row_pos = (me * ROWS + lax.broadcasted_iota(jnp.int32, (ROWS, COLS), 0)).astype(F32)
    col_pos = (side * COLS + lax.broadcasted_iota(jnp.int32, (ROWS, COLS), 1)).astype(F32)
    across = 4.0 * (row_pos + 0.5) / (ROWS * N_ROLL) - 2.5
    transverse = 4.0 * (col_pos + 0.5) / (COLS * N_SIDE) - 2.0
    ground = offset[0] + 0.5 * across * across + 0.5 * transverse * transverse
    args[6].wait()
    ripple = ROUGH_STEP * rough[...].astype(F32)
    settle(p6s.at[rest], p6r.at[rest], 14)
    for h in range(2):
        lanes = slice(128 * h, 128 * h + 128)
        bend = p6r[pl.ds(32 * h, 32)].reshape(128, 128)
        film[:, lanes] = ground[:, lanes] + bend - ripple[:, lanes]


def per_device(pressure, source, coupling, binv, lower, mask, rough, offset):
    consts = [jnp.asarray(t) for t in tables()]
    hbm = pl.BlockSpec(memory_space=pl.ANY)
    f = lambda *shape: pltpu.VMEM(shape, F32)
    b = lambda *shape: pltpu.VMEM(shape, BF16)
    i32 = lambda *shape: pltpu.VMEM(shape, jnp.int32)
    scratch = [
        f(128, 256), f(128, 256), f(128, 256), f(128, 128), f(1, 256), i32(1, 256), i32(128, 256),
        b(512, 768), b(256, 1536), b(1536, 512), b(1536, 512),
        f(2, 256, 256), f(2, 256), f(2, 16, 256),
        f(2, 32, 128), f(2, 32, 128), f(2, 128, 128),
        f(2, 5, 128), f(64, 5, 128), f(4, 128), f(2, 3, 128), f(64, 4, 128), f(2, 64, 3, 128),
        f(64, 3, 128), f(64, 3, 128), f(8, 3, 128), f(8, 3, 128), f(64, 3, 128), f(64, 1, 128),
        f(64, 1, 128), f(8, 1, 128), f(128, 128), f(32, 4, 128), f(64, 4, 128),
        f(64, 1, 128), f(1, 128),
        b(128, 384), b(128, 768), f(128, 256),
        f(2, 144, 256), b(256, 768), b(256, 768),
        f(64, 5, 128), f(64, 5, 128), f(64, 4, 128), b(768, 128), f(64, 8, 128), f(64, 8, 128),
        b(768, 256), f(2, 8, 16, 256), f(2, 8, 16, 256), b(144, 1536), f(2, 2, 8, 16, 128),
        f(2, 2, 8, 16, 128), f(64, 8, 128), f(64, 8, 128), b(1536, 128), f(64, 4, 128),
        f(64, 4, 128),
        pltpu.SemaphoreType.DMA((7,)), pltpu.SemaphoreType.DMA((7,)), pltpu.SemaphoreType.REGULAR,
        pltpu.SemaphoreType.DMA((2, 2)), pltpu.SemaphoreType.DMA((2, 2)),
        pltpu.SemaphoreType.DMA((15,)), pltpu.SemaphoreType.DMA((15,)),
    ]
    out = pltpu.VMEM((ROWS, COLS), F32)
    return pl.pallas_call(
        main_kernel,
        out_shape=(out, out),
        in_specs=[hbm] * 7 + [pl.BlockSpec(memory_space=pltpu.SMEM)] + [hbm] * 7,
        out_specs=(pl.BlockSpec(memory_space=pltpu.VMEM),) * 2,
        scratch_shapes=scratch,
        compiler_params=pltpu.CompilerParams(
            collective_id=0, has_side_effects=True, vmem_limit_bytes=56 * 1024 * 1024
        ),
    )(pressure, source, coupling, binv, lower, mask, rough, offset, *consts)


def solution(mesh):
    spec = P("roll", "side")
    return jax.shard_map(
        per_device,
        mesh=mesh,
        in_specs=(spec,) * 7 + (P(),),
        out_specs=(spec, spec),
        check_vma=False,
    )
```

```python
import functools
import math

import jax
import jax.numpy as jnp
import ml_dtypes
import numpy as np
from jax import lax
from jax.experimental import pallas as pl
from jax.experimental.pallas import tpu as pltpu
from jax.sharding import PartitionSpec as P

SWEEPS = 4
ROUGH_STEP = 0.05
MESH = pl.DeviceIdType.MESH
F32 = jnp.float32
BF16 = jnp.bfloat16

N_ROLL, N_SIDE = 64, 8
ROWS, COLS = 128, 256
FFT_X, FFT_Y = 2 * N_ROLL * ROWS, 2 * N_SIDE * COLS
CLASSES = N_SIDE + 1


def split_np(x):
    x = x.astype(np.float32)
    hi = x.astype(ml_dtypes.bfloat16)
    lo = (x - hi.astype(np.float32)).astype(ml_dtypes.bfloat16)
    return hi, lo


def wide_np(x, axis):
    hi, lo = split_np(x)
    return np.concatenate([hi, hi, lo], axis=axis)


def turns(ints, length):
    return 2.0 * np.pi * (ints % length).astype(np.float64) / length


@functools.lru_cache(None)
def tables():
    a = np.arange(N_ROLL)
    ang = turns(a[:, None] * a[None, :], 2 * N_ROLL)
    sect = np.stack([np.cos(ang), -np.sin(ang)], axis=1)
    sect[0, 1] = np.where(a % 2 == 0, 1.0, -1.0)
    sect = np.einsum("uca,ij->uciaj", sect, np.eye(4)).reshape(8 * N_ROLL, 4 * N_ROLL)
    c = np.arange(COLS)
    ang = turns(c[:, None] * c[None, :], COLS)
    dcos, dsin = np.cos(ang), np.sin(ang)
    dft = np.block([[dcos, -dsin], [dsin, dcos]])
    v1 = np.arange(16)
    ang = turns(v1[:, None] * c[None, :], FFT_Y)
    twiddle = np.stack([np.cos(ang), np.sin(ang)]).astype(np.float32)
    q = np.arange(ROWS).reshape(N_SIDE, 16)
    t = np.arange(ROWS).reshape(32, 4)
    ang = turns(q[:, :, None, None] * t[None, None], ROWS)
    cb, sb = np.cos(ang), np.sin(ang)
    main = np.zeros((2, 2, 2, N_SIDE, 16, 32, 2, 4))
    main[1, 0, 0, :, :, :, 0], main[1, 0, 0, :, :, :, 1] = cb, sb
    main[1, 0, 1, :, :, :, 0], main[1, 0, 1, :, :, :, 1] = -sb, cb
    main[1, 1, 0, :, :, :, 0], main[1, 1, 0, :, :, :, 1] = -sb, cb
    main[1, 1, 1, :, :, :, 0], main[1, 1, 1, :, :, :, 1] = -cb, -sb
    even = np.where(q <= 64, q, q - 64)
    ang = turns(even[:, :, None, None] * t[None, None], ROWS)
    main[0, 0, 0, :, :, :, 0] = np.where((q <= 64)[:, :, None, None], np.cos(ang), np.sin(ang))
    odd = 64 + 128 * np.where(q < 64, q, q - 64)
    ang = turns(odd[:, :, None, None] * t[None, None], FFT_X)
    main[0, 0, 1, :, :, :, 1] = np.where((q < 64)[:, :, None, None], np.cos(ang), np.sin(ang))
    main = main.reshape(2, 2, 256, 256).astype(np.float32)
    cols_t = np.broadcast_to(t[:, None, :], (32, 2, 4)).reshape(256)
    ang = turns(a[:, None] * cols_t[None, :], FFT_X)
    slant = np.stack([np.cos(ang), np.sin(ang)], axis=1).astype(np.float32)
    return (
        wide_np(sect, 1),
        wide_np(sect.T, 1),
        wide_np(dft, 0),
        wide_np(dft.T, 0),
        main,
        slant,
        twiddle,
    )


def split(x):
    hi = x.astype(BF16)
    return hi, (x - hi.astype(F32)).astype(BF16)


def mm(a, b):
    return jnp.dot(a, b, preferred_element_type=F32)


def place(device):
    return lax.rem(device, 2) * 32 + lax.div(device, 2)


def combine(terms):
    total = None
    for coef, value in terms:
        if abs(coef) < 1e-12:
            continue
        if abs(coef - 1.0) < 1e-12:
            total = value if total is None else total + value
        elif abs(coef + 1.0) < 1e-12:
            total = -value if total is None else total - value
        else:
            total = coef * value if total is None else total + coef * value
    return total


def far(i, x, z, c):
    m, n = lax.div(i, 8), lax.div(lax.rem(i, 8), 2)
    dz = 4 + lax.div(m + 1, 2) * (1 - 2 * lax.rem(m, 2))
    dx = 2 + lax.div(n + 1, 2) * (1 - 2 * lax.rem(n, 2))
    return (
        lax.rem(x + dx, 4) * 16 + lax.rem(z + dz, 8) * 2 + lax.rem(c + 1 - lax.rem(i, 2), 2)
    )


def main_kernel(
    press_h, source_h, coupling_h, binv_h, lower_h, mask_h, rough_h, offset,
    w3_h, wt3_h, d3_h, dt3_h, main_h, slant_h, twid_h,
    newp, film,
    press, source, coupling, binv, lower, mask, rough,
    w3, wt3, d3, dt3, maint, slant, twid,
    pack, halo, bhalo,
    cs, cr, outs0, outs, recv0, recv, gfull, gpre, gall, cgroup, carry_buf, gsel, gsel_pre, gsel_all, bt, btt, bx, carry4, partner,
    b3, be3, loc4,
    kern, m3, mt3,
    p1s, p1r, qf, q3, p2s, p2r, x3, us, yb, zs, ob, ub, p5s, p5r, v3, p6s, p6r,
    const_sem, arg_sem, known, halo_ss, halo_rs, ss, rs,
):
    me = lax.axis_index("roll")
    side = lax.axis_index("side")
    along_x, along_z, half = lax.div(me, 16), lax.rem(lax.div(me, 2), 8), lax.rem(me, 2)
    group = lax.div(me, 2)
    other = me + 1 - 2 * half
    barrier = pltpu.get_barrier_semaphore()

    def greet(sem, where):
        pl.semaphore_signal(sem, inc=1, device_id=where, device_id_type=MESH)

    def plane(i):
        n = lax.div(i, 2)
        dx = 2 + lax.div(n + 1, 2) * (1 - 2 * lax.rem(n, 2))
        core = lax.rem(half + 1 - lax.rem(i, 2), 2)
        return lax.rem(along_x + dx, 4) * 16 + along_z * 2 + core

    for d in (4, 3, 5, 2, 6, 1, 7):
        greet(barrier, {"roll": along_x * 16 + lax.rem(along_z + d, 8) * 2 + half})
        greet(barrier, {"side": lax.rem(side + d, N_SIDE)})
    for i in range(7):
        greet(barrier, {"roll": plane(i)})

    variant = jnp.minimum(me, 1)
    loads = [
        pltpu.make_async_copy(s, d, const_sem.at[i])
        for i, (s, d) in enumerate(
            [
                (w3_h, w3), (wt3_h, wt3), (d3_h, d3), (dt3_h, dt3),
                (main_h.at[variant], maint), (slant_h.at[me], slant), (twid_h, twid),
            ]
        )
    ]
    args = [
        pltpu.make_async_copy(s, d, arg_sem.at[i])
        for i, (s, d) in enumerate(
            [
                (press_h, press), (source_h, source), (coupling_h, coupling), (binv_h, binv),
                (lower_h, lower), (mask_h, mask), (rough_h, rough),
            ]
        )
    ]
    for load in args:
        load.start()
    for load in loads:
        load.start()

    def push(src, dst, phase, where):
        pltpu.make_async_remote_copy(
            src_ref=src, dst_ref=dst, send_sem=ss.at[phase], recv_sem=rs.at[phase],
            device_id=where, device_id_type=MESH,
        ).start()

    def send_roll(src_at, dst, phase):
        def body(i, _):
            to = far(i, along_x, along_z, half)
            push(src_at(to), dst, phase, {"roll": to})
            return 0

        lax.fori_loop(0, N_ROLL - 1, body, 0, unroll=63)

    def send_side(src_at, dst, phase):
        for d in (4, 3, 5, 2, 6, 1, 7):
            to = lax.rem(side + d, N_SIDE)
            push(src_at(to), dst, phase, {"side": to})

    def settle(src, dst, phase):
        pltpu.make_async_remote_copy(
            src_ref=src, dst_ref=dst, send_sem=ss.at[phase], recv_sem=rs.at[phase],
            device_id={"roll": other}, device_id_type=MESH,
        ).wait()

    rest = pl.ds(0, N_ROLL - 1)
    rest_side = pl.ds(0, N_SIDE - 1)

    lane_b = lax.broadcasted_iota(jnp.int32, (ROWS, 128), 1)
    for load in args[:6]:
        load.wait()
    for i, ref in enumerate((press, source, coupling)):
        pack[0, pl.ds(8 * i, 8), :] = ref[:, 0:128].T[0:8]
        pack[1, pl.ds(8 * i, 8), :] = ref[:, 128:256].T[120:128]
    for j in range(2):
        lanes = slice(128 * j, 128 * j + 128)
        pack[j, pl.ds(24, 8), :] = jnp.concatenate(
            [lower[:, lanes], mask[:, lanes].astype(F32), jnp.zeros((6, 128), F32)], axis=0
        )
    gain_m = binv[127:128, 0:1] * lower[...]
    first_row = binv[...].T[0:1]
    for j in range(2):
        lanes = slice(128 * j, 128 * j + 128)
        cs[j, 0:1, :] = gain_m[:, 0:128]
        cs[j, 1:2, :] = gain_m[:, 128:256]
        cs[j, 2:3, :] = lower[:, lanes]
        cs[j, 3:4, :] = mask[:, lanes].astype(F32)
        cs[j, 4:5, :] = first_row
    pl.semaphore_wait(barrier, 21)
    halo_copies = []
    for k in range(2):
        for j, d in ((0, N_SIDE - 1), (1, 1)):
            to = lax.rem(side + d, N_SIDE)
            s, dst = ((pack.at[j], halo.at[j]), (binv, bhalo.at[j]))[k]
            c = pltpu.make_async_remote_copy(
                src_ref=s, dst_ref=dst, send_sem=halo_ss.at[j, k], recv_sem=halo_rs.at[j, k],
                device_id={"side": to}, device_id_type=MESH,
            )
            c.start()
            halo_copies.append(c)
    for i in range(7):
        greet(known, {"roll": plane(i)})
    cr[me] = cs[half]
    bhi, blo = split(binv[...])
    b3[:, 0:128] = bhi
    b3[:, 128:256] = bhi
    b3[:, 256:384] = blo
    pl.semaphore_wait(known, 7)
    send_roll(lambda to: cs.at[lax.rem(to, 2)], cr.at[me], 0)
    halo_copies[0].wait()
    halo_copies[1].wait()
    has_right = side < N_SIDE - 1
    has_left = side > 0
    is_right = lane_b < 64
    valid = jnp.logical_or(
        jnp.logical_and(is_right, has_right), jnp.logical_and(jnp.logical_not(is_right), has_left)
    )
    ext = []
    for i in range(3):
        tall = jnp.concatenate(
            [halo[0, pl.ds(8 * i, 8), :], jnp.zeros((112, 128), F32), halo[1, pl.ds(8 * i, 8), :]],
            axis=0,
        )
        ext.append(jnp.where(valid, tall.T, 0.0))
    row_right = is_right[0:1]
    row_valid = valid[0:1]
    lower_e = jnp.where(row_valid, jnp.where(row_right, halo[0, 24:25, :], halo[1, 24:25, :]), 0.0)
    mask_e = jnp.where(row_right, halo[0, 25:26, :], halo[1, 25:26, :]) > 0.5
    first = binv[:, 0:1]
    lower_w = jnp.concatenate([lower[...], lower_e], axis=1)
    mask_w = jnp.concatenate([mask[...].astype(F32), mask_e.astype(F32)], axis=1) > 0.5
    source_w = jnp.concatenate([source[...], ext[1]], axis=1)
    coupling_w = jnp.concatenate([coupling[...], ext[2]], axis=1)
    field = jnp.concatenate([press[...], ext[0]], axis=1)

    for sweep in range(SWEEPS - 1):
        rhs = source_w + coupling_w * (pltpu.roll(field, 1, 1) + pltpu.roll(field, 383, 1))
        hi, lo = split(rhs[:, :256])
        stack = jnp.concatenate([hi, lo, hi], axis=0)
        he = rhs[:, 256:]
        hr, lr = split(jnp.where(is_right, he, 0.0))
        hl, ll = split(jnp.where(is_right, 0.0, he))
        stack_e = jnp.concatenate([hr, hl, lr, ll, hr, hl], axis=0)
        tail = mm(b3[112:128, :], stack)
        if sweep == 0:
            halo_copies[2].wait()
            halo_copies[3].wait()
            rhi, rlo = split(bhalo[0])
            lhi, llo = split(bhalo[1])
            for i, part in enumerate((rhi, lhi, rhi, lhi, rlo, llo)):
                be3[:, pl.ds(128 * i, 128)] = part
            first_e = jnp.where(is_right, bhalo[0, :, 0:1], bhalo[1, :, 0:1])
            first_w = jnp.concatenate([jnp.broadcast_to(first, (ROWS, COLS)), first_e], axis=1)
            outs0[3:4, :] = first_e[127:128] * lower_e
        tail_e = mm(be3[112:128, :], stack_e)
        out = outs0 if sweep == 0 else outs.at[sweep - 1]
        for i in range(3):
            row = tail_e[15:16] if i == 2 else tail[15:16, 128 * i : 128 * i + 128]
            out[i : i + 1, :] = row
        into = recv0 if sweep == 0 else recv.at[sweep - 1]
        send_roll(lambda to: out, into.at[me], 1 + sweep)
        local = jnp.concatenate([mm(b3[...], stack), mm(be3[...], stack_e)], axis=1)
        if sweep == 0:
            i = lax.broadcasted_iota(jnp.int32, (16, COLS), 0)
            q = 16 * side + i
            lane = lax.broadcasted_iota(jnp.int32, (16, COLS), 1)
            reach = min(FFT_X, FFT_Y) / 16.0
            scale = 0.4 * reach / (float(FFT_X) * float(FFT_Y))
            for part in range(2):
                if part == 0:
                    u_first = 128 * jnp.where(q <= 64, q, q - 64)
                    single = jnp.logical_and(me == 0, jnp.logical_or(q == 0, q == 64))
                    weight = jnp.where(single, scale, 2.0 * scale)
                else:
                    u_first = 64 + 128 * jnp.where(q < 64, q, q - 64)
                    weight = jnp.full((16, COLS), 2.0 * scale, F32)
                u = jnp.where(me == 0, u_first, me + 128 * q)
                fu = jnp.minimum(u, FFT_X - u).astype(F32) / FFT_X
                fu2 = fu * fu
                for v1 in range(CLASSES):
                    v = v1 + 16 * lane
                    fv = jnp.minimum(v, FFT_Y - v).astype(F32) / FFT_Y
                    w = weight if v1 in (0, 8) else 2.0 * weight
                    kern[part, pl.ds(16 * v1, 16), :] = w / (
                        1.0 + reach * jnp.sqrt(fu2 + fv * fv)
                    )
            settle(cr.at[rest], cr.at[rest], 0)
            gfull[:, 0:2, :] = cr[:, 0:2, :]
        if sweep == 1:
            loads[4].wait()
            loads[5].wait()
            mrow = maint[0] * slant[0:1, :] + maint[1] * slant[1:2, :]
            hi, lo = split(mrow)
            m3[:, 0:256] = hi
            m3[:, 256:512] = hi
            m3[:, 512:768] = lo
            bt[...] = jnp.zeros_like(bt)
            for a in range(N_ROLL):
                bt[a : a + 1, :] = cr[a, 4:5, :]
                gain = jnp.where(half == 0, cr[a, 0:1, :], cr[a, 1:2, :])
                gsel[a] = gain
                gsel_pre[a] = jnp.ones((1, 128), F32) if a % 8 == 0 else product
                product = gain if a % 8 == 0 else product * gain
                if a % 8 == 7:
                    gsel_all[a // 8] = product
        if sweep == 2:
            mrow = maint[0] * slant[0:1, :] + maint[1] * slant[1:2, :]
            hi, lo = split(mrow.T)
            mt3[:, 0:256] = hi
            mt3[:, 256:512] = hi
            mt3[:, 512:768] = lo
            btt[...] = bt[...].T.reshape(32, 4, 128)
            mine = btt[group]
            for a in range(N_ROLL):
                bx[a] = jnp.broadcast_to(mine[:, a : a + 1], (4, 128))
        settle(into.at[rest], into.at[rest], 1 + sweep)
        if sweep == 0:
            gfull[:, 2:3, :] = recv0[:, 3:4, :]

        totals = []
        for g in range(8):
            c = flow = None
            for j in range(8):
                k = 8 * g + j
                flow = recv0[k, 0:3] if sweep == 0 else recv[sweep - 1, k]
                gain = gfull[k]
                carry_buf[k] = jnp.zeros((3, 128), F32) if c is None else c
                c = flow if c is None else flow + gain * c
                if sweep == 0:
                    gpre[k] = jnp.ones((3, 128), F32) if j == 0 else product
                    product = gain if j == 0 else product * gain
            if sweep == 0:
                gall[g] = product
            totals.append(c)
        c = jnp.zeros((3, 128), F32)
        for g in range(8):
            cgroup[g] = c
            c = totals[g] + gall[g] * c
        mine = carry_buf[me] + gpre[me] * cgroup[lax.div(me, 8)]
        carry = jnp.concatenate([mine[0:1], mine[1:2], mine[2:3]], axis=1)
        solved = local + first_w * (lower_w * carry)
        field = jnp.where(mask_w, jnp.maximum(solved, 0.0), solved)

    rhs = source_w + coupling_w * (pltpu.roll(field, 1, 1) + pltpu.roll(field, 383, 1))
    hi, lo = split(rhs[:, :256])
    local = mm(b3[...], jnp.concatenate([hi, lo, hi], axis=0))
    for h in range(2):
        tile = local[:, 128 * h : 128 * h + 128]
        p1s[pl.ds(32 * h, 32), 0:4, :] = tile.reshape(32, 4, 128)
        p1s[pl.ds(32 * h, 32), 4:5, :] = jnp.broadcast_to(tile[127:128].reshape(1, 1, 128), (32, 1, 128))
    send_roll(lambda to: p1s.at[place(to)], p1r.at[me], 4)
    p1r[me] = p1s[place(me)]
    loc4[...] = local
    loads[0].wait()
    settle(p1s.at[rest], p1r.at[rest], 4)

    inner, totals = [], []
    for g in range(8):
        c = None
        for j in range(8):
            k = 8 * g + j
            inner.append(c)
            flow = p1r[k, 4:5, :]
            c = flow if c is None else flow + gsel[k] * c
        totals.append(c)
    c = jnp.zeros((1, 128), F32)
    for g in range(8):
        for j in range(8):
            k = 8 * g + j
            ck = c if j == 0 else inner[k] + gsel_pre[k] * c
            carry4[k] = ck
            sol = p1r[k, 0:4, :] + bx[k] * (cr[k, 2:3, :] * ck)
            qf[k] = jnp.where(cr[k, 3:4, :] > 0.5, jnp.maximum(sol, 0.0), sol)
        c = totals[g] + gsel_all[g] * c
    hi, lo = split(qf[...].reshape(256, 128))
    q3[0:256] = hi
    q3[256:512] = lo
    q3[512:768] = hi
    p2s[...] = mm(w3[...], q3[...]).reshape(64, 8, 128)

    send_roll(lambda to: p2s.at[to], p2r.at[place(me)], 5)
    push(carry4.at[other], partner, 6, {"roll": other})
    p2r[place(me)] = p2s[me]
    settle(carry4.at[0], partner, 6)
    for h in range(2):
        lanes = slice(128 * h, 128 * h + 128)
        carry = jnp.where(half == h, carry4[me], partner[...])
        sol = loc4[:, lanes] + binv[:, 0:1] * (lower[:, lanes] * carry)
        newp[:, lanes] = jnp.where(mask[:, lanes] == 1, jnp.maximum(sol, 0.0), sol)
    settle(p2s.at[rest], p2r.at[rest], 5)
    for h in range(2):
        hi, lo = split(p2r[pl.ds(32 * h, 32)].reshape(256, 128))
        lanes = slice(128 * h, 128 * h + 128)
        x3[0:256, lanes] = hi
        x3[256:512, lanes] = lo
        x3[512:768, lanes] = hi

    for part in range(2):
        us[part] = mm(m3[128 * part : 128 * part + 128, :], x3[...]).reshape(8, 16, 256)
        send_side(lambda to: us.at[part, to], yb.at[part, side], 7 + part)
        yb[part, side] = us[part, side]
    loads[2].wait()
    loads[3].wait()
    loads[6].wait()

    cosines = [[math.cos(math.pi * s * v / 8.0) for v in range(9)] for s in range(8)]
    sines = [[math.sin(math.pi * s * v / 8.0) for v in range(9)] for s in range(8)]

    def put(v1, lanes, re, im):
        at = 16 * v1
        for which, value in ((0, re), (256, im)):
            hi, lo = split(value)
            zs[pl.ds(at, 16), pl.ds(which + lanes, 128)] = hi
            zs[pl.ds(at, 16), pl.ds(512 + which + lanes, 128)] = lo
            zs[pl.ds(at, 16), pl.ds(1024 + which + lanes, 128)] = hi

    for part in range(2):
        settle(us.at[part, rest_side], yb.at[part, rest_side], 7 + part)
        for lanes in (0, 128):
            x = [yb[part, s, :, pl.ds(lanes, 128)] for s in range(8)]
            for v in range(5):
                er = combine([(cosines[s][v], x[s]) for s in (0, 2, 4, 6)])
                orr = combine([(cosines[s][v], x[s]) for s in (1, 3, 5, 7)])
                ei = combine([(-sines[s][v], x[s]) for s in (0, 2, 4, 6)])
                oi = combine([(-sines[s][v], x[s]) for s in (1, 3, 5, 7)])
                zero = jnp.zeros((16, 128), F32)
                ei = zero if ei is None else ei
                oi = zero if oi is None else oi
                orr = zero if orr is None else orr
                todo = [(v, er + orr, ei + oi)]
                if v < 4:
                    todo.append((8 - v, er - orr, oi - ei))
                for v1, yr, yi in todo:
                    c = twid[0, v1 : v1 + 1, lanes : lanes + 128]
                    s = twid[1, v1 : v1 + 1, lanes : lanes + 128]
                    put(v1, lanes, yr * c + yi * s, yi * c - yr * s)
        spec = mm(zs[...], d3[...])
        for v1 in range(CLASSES):
            at = 16 * v1
            for lanes in (0, 128):
                k = kern[part, pl.ds(at, 16), pl.ds(lanes, 128)]
                put(
                    v1, lanes,
                    spec[at : at + 16, lanes : lanes + 128] * k,
                    spec[at : at + 16, 256 + lanes : 384 + lanes] * k,
                )
        back = mm(zs[...], dt3[...])
        for lanes in (0, 128):
            yr, yi = [], []
            for v1 in range(CLASSES):
                at = 16 * v1
                zr = back[at : at + 16, lanes : lanes + 128]
                zi = back[at : at + 16, 256 + lanes : 384 + lanes]
                c = twid[0, v1 : v1 + 1, lanes : lanes + 128]
                s = twid[1, v1 : v1 + 1, lanes : lanes + 128]
                yr.append(zr * c - zi * s)
                yi.append(zr * s + zi * c)
            plus_r = [yr[v] + yr[8 - v] for v in range(4)] + [yr[4]]
            plus_i = [yi[v] + yi[8 - v] for v in range(4)] + [yi[4]]
            less_r = [yr[v] - yr[8 - v] for v in range(4)] + [yr[4]]
            less_i = [yi[v] - yi[8 - v] for v in range(4)] + [yi[4]]
            h = lanes // 128
            for s in range(8):
                re, im = (plus_r, less_i) if s % 2 == 0 else (less_r, plus_i)
                ob[h, part, s] = combine(
                    [(cosines[s][v], re[v]) for v in range(5)]
                    + [(-sines[s][v], im[v]) for v in range(5)]
                )
            send_side(lambda to: ob.at[h, part, to], ub.at[h, part, side], 9 + 2 * h + part)
            ub[h, part, side] = ob[h, part, side]

    for h in range(2):
        for part in range(2):
            settle(ob.at[h, part, rest_side], ub.at[h, part, rest_side], 9 + 2 * h + part)
        hi, lo = split(ub[h].reshape(256, 128))
        v3[0:256] = hi
        v3[256:512] = lo
        v3[512:768] = hi
        p5s[pl.ds(32 * h, 32)] = mm(mt3[...], v3[0:768]).reshape(32, 8, 128)

        def body(i, _):
            to = far(2 * i + 1, along_x, along_z, h)
            push(p5s.at[place(to)], p5r.at[me], 13, {"roll": to})
            return 0

        lax.fori_loop(0, 31, body, 0)

        @pl.when(half != h)
        def _():
            push(p5s.at[place(other)], p5r.at[me], 13, {"roll": other})

    p5r[me] = p5s[place(me)]
    loads[1].wait()
    settle(p5s.at[rest], p5r.at[rest], 13)
    hi, lo = split(p5r[...].reshape(512, 128))
    v3[0:512] = hi
    v3[512:1024] = lo
    v3[1024:1536] = hi
    p6s[...] = mm(wt3[...], v3[...]).reshape(64, 4, 128)

    send_roll(lambda to: p6s.at[to], p6r.at[place(me)], 14)
    p6r[place(me)] = p6s[me]
    row_pos = (me * ROWS + lax.broadcasted_iota(jnp.int32, (ROWS, COLS), 0)).astype(F32)
    col_pos = (side * COLS + lax.broadcasted_iota(jnp.int32, (ROWS, COLS), 1)).astype(F32)
    across = 4.0 * (row_pos + 0.5) / (ROWS * N_ROLL) - 2.5
    transverse = 4.0 * (col_pos + 0.5) / (COLS * N_SIDE) - 2.0
    ground = offset[0] + 0.5 * across * across + 0.5 * transverse * transverse
    args[6].wait()
    ripple = ROUGH_STEP * rough[...].astype(F32)
    settle(p6s.at[rest], p6r.at[rest], 14)
    for h in range(2):
        lanes = slice(128 * h, 128 * h + 128)
        bend = p6r[pl.ds(32 * h, 32)].reshape(128, 128)
        film[:, lanes] = ground[:, lanes] + bend - ripple[:, lanes]


def per_device(pressure, source, coupling, binv, lower, mask, rough, offset):
    consts = [jnp.asarray(t) for t in tables()]
    hbm = pl.BlockSpec(memory_space=pl.ANY)
    f = lambda *shape: pltpu.VMEM(shape, F32)
    b = lambda *shape: pltpu.VMEM(shape, BF16)
    i32 = lambda *shape: pltpu.VMEM(shape, jnp.int32)
    scratch = [
        f(128, 256), f(128, 256), f(128, 256), f(128, 128), f(1, 256), i32(1, 256), i32(128, 256),
        b(512, 768), b(256, 1536), b(1536, 512), b(1536, 512),
        f(2, 256, 256), f(2, 256), f(2, 16, 256),
        f(2, 32, 128), f(2, 32, 128), f(2, 128, 128),
        f(2, 5, 128), f(64, 5, 128), f(4, 128), f(2, 3, 128), f(64, 4, 128), f(2, 64, 3, 128),
        f(64, 3, 128), f(64, 3, 128), f(8, 3, 128), f(8, 3, 128), f(64, 3, 128), f(64, 1, 128),
        f(64, 1, 128), f(8, 1, 128), f(128, 128), f(32, 4, 128), f(64, 4, 128),
        f(64, 1, 128), f(1, 128),
        b(128, 384), b(128, 768), f(128, 256),
        f(2, 144, 256), b(256, 768), b(256, 768),
        f(64, 5, 128), f(64, 5, 128), f(64, 4, 128), b(768, 128), f(64, 8, 128), f(64, 8, 128),
        b(768, 256), f(2, 8, 16, 256), f(2, 8, 16, 256), b(144, 1536), f(2, 2, 8, 16, 128),
        f(2, 2, 8, 16, 128), f(64, 8, 128), f(64, 8, 128), b(1536, 128), f(64, 4, 128),
        f(64, 4, 128),
        pltpu.SemaphoreType.DMA((7,)), pltpu.SemaphoreType.DMA((7,)), pltpu.SemaphoreType.REGULAR,
        pltpu.SemaphoreType.DMA((2, 2)), pltpu.SemaphoreType.DMA((2, 2)),
        pltpu.SemaphoreType.DMA((15,)), pltpu.SemaphoreType.DMA((15,)),
    ]
    out = pltpu.VMEM((ROWS, COLS), F32)
    return pl.pallas_call(
        main_kernel,
        out_shape=(out, out),
        in_specs=[hbm] * 7 + [pl.BlockSpec(memory_space=pltpu.SMEM)] + [hbm] * 7,
        out_specs=(pl.BlockSpec(memory_space=pltpu.VMEM),) * 2,
        scratch_shapes=scratch,
        compiler_params=pltpu.CompilerParams(
            collective_id=0, has_side_effects=True, vmem_limit_bytes=56 * 1024 * 1024
        ),
    )(pressure, source, coupling, binv, lower, mask, rough, offset, *consts)


def solution(mesh):
    spec = P("roll", "side")
    return jax.shard_map(
        per_device,
        mesh=mesh,
        in_specs=(spec,) * 7 + (P(),),
        out_specs=(spec, spec),
        check_vma=False,
    )
```
